32 devices in a mesh: seq: 2 (over core), batch: 16 (over z, y, x).
Axes of the slice: x: 2, y: 2, z: 4, core: 2. Of those that a mesh axis runs over, the one named last changes fastest.
Arguments:
- inputs: bfloat16 [64, 512, 512], P('batch', 'seq'), may hold values from -6 to 6
- conv_weight: bfloat16 [9, 512, 512], replicated, may hold values from -0.09375 to 0.09375
- conv_bias: float32 [512], replicated, may hold values from -1.5 to 1.5
- norm1_gain: float32 [512], replicated, may hold values from 0.25 to 1.75
- norm1_shift: float32 [512], replicated, may hold values from -1.5 to 1.5
- norm2_gain: float32 [512], replicated, may hold values from 0.25 to 1.75
- norm2_shift: float32 [512], replicated, may hold values from -1.5 to 1.5
- up_weight: bfloat16 [512, 2048], replicated, may hold values from -0.25 to 0.25
- up_bias: float32 [2048], replicated, may hold values from -1.5 to 1.5
- down_weight: bfloat16 [2048, 512], replicated, may hold values from -0.1875 to 0.1875
- down_bias: float32 [512], replicated, may hold values from -1.5 to 1.5
- head_weight: bfloat16 [512, 6], replicated, may hold values from -0.59765625 to 0.59765625
- species: int32 [64], P('batch'), may hold values from 0 to 7
- cotangent: bfloat16 [64, 512, 512], P('batch', 'seq'), may hold values from -6 to 6
Outputs:
- activations: bfloat16 [64, 512, 512], P('batch', 'seq')
- input_grad: bfloat16 [64, 512, 512], P('batch', 'seq')
- conv_weight_grad: float32 [9, 512, 512], replicated
- conv_bias_grad: float32 [512], replicated
- norm1_gain_grad: float32 [512], replicated
- norm1_shift_grad: float32 [512], replicated
- norm2_gain_grad: float32 [512], replicated
- norm2_shift_grad: float32 [512], replicated
- up_weight_grad: float32 [512, 2048], replicated
- up_bias_grad: float32 [2048], replicated
- down_weight_grad: float32 [2048, 512], replicated
- down_bias_grad: float32 [512], replicated
- frequencies: float32 [8, 6], replicated
The draws below stay inside these ranges and needn't reach their ends.
All inputs are finite; a program needn't handle non-finite values.
Results may differ from the reference program's by a relative error of at most 0.0062.
Values may be sent and summed in bfloat16 or wider, within the bound.
No kernel may reach another device: no remote copies, remote signals or barrier semaphores. Data moves between devices by JAX's collectives and lax.ppermute only.
A program may use at most 128 MiB of HBM per device.

```python
import math
import jax
import jax.numpy as jnp
import numpy as np
from jax import lax

D = 512
FF = 2048
KER = 9
DILATION_STEP = 8
WINDOW_BASES = 512
WIN_DEV = 4
SPECIES = 8
RIM = 32
WINDOWS = 64


def plant(drawn, own_key, smallest, high):
    index_at = [jax.random.randint(jax.random.fold_in(own_key, axis), (), 0, length) for axis, length in enumerate(drawn.shape)]
    longest = drawn.shape.index(max(drawn.shape))
    next_to = index_at[:longest] + [(index_at[longest] + 1) % drawn.shape[longest]] + index_at[longest + 1:]
    return drawn.at[tuple(index_at)].set(smallest).at[tuple(next_to)].set(high)


def shard_levels(rng, extent, pieces, smallest, largest):
    loudness = 1.0
    for axis_at, blocks in pieces:
        steps = jax.random.uniform(jax.random.fold_in(jax.random.fold_in(rng, 6), axis_at), (blocks,), jnp.float32, smallest / len(pieces), largest / len(pieces))
        loudness = loudness * jnp.repeat(jnp.exp(steps), extent[axis_at] // blocks).reshape((-1,) + (1,) * (len(extent) - 1 - axis_at))
    return loudness


def rank_table(number_of, lean):
    portions = [(1 << 20) // math.isqrt(grade ** lean) + 1 for grade in range(1, number_of + 1)]
    width = 1 + sum(portions) // (1 << 30)
    return np.cumsum(np.array([max(1, weight // width) for weight in portions]))


def ranked_ids(own_key, shape, count, slope):
    listing = rank_table(count, slope)
    lot = jax.random.randint(jax.random.fold_in(own_key, 1), shape, 0, int(listing[count - 1]))
    standing = jnp.searchsorted(jnp.asarray(listing, jnp.int32), lot, side="right")
    return jax.random.permutation(jax.random.fold_in(own_key, 2), count)[standing].astype(jnp.int32)


def normal_values(rng, extent, deviation, limit, split=(), kind=jnp.bfloat16):
    level = shard_levels(rng, extent, split, -0.22, 0.18) if split else 1.0
    result = jax.random.normal(rng, extent, jnp.float32) * deviation * level
    return jnp.minimum(jnp.maximum(result, -limit), limit).astype(kind)


def setup_inputs(seed: int = 0) -> dict:
    key_of = jax.random.split(jax.random.key(seed), 15)
    inputs = normal_values(key_of[0], (WINDOWS, WINDOW_BASES, D), 1.0, 6.0, ((0, 16), (1, 2)))
    conv_weight = normal_values(key_of[1], (KER, D, D), (KER * D) ** -0.5, 0.09375)
    conv_bias = normal_values(key_of[2], (D,), 0.3, 1.5, (), jnp.float32)
    norm1_gain = jnp.clip(1.0 + 0.15 * jax.random.normal(key_of[3], (D,), jnp.float32), 0.25, 1.75)
    norm1_shift = normal_values(key_of[4], (D,), 0.3, 1.5, (), jnp.float32)
    norm2_gain = jnp.clip(1.0 + 0.15 * jax.random.normal(key_of[5], (D,), jnp.float32), 0.25, 1.75)
    norm2_shift = normal_values(key_of[6], (D,), 0.3, 1.5, (), jnp.float32)
    up_weight = normal_values(key_of[7], (D, FF), D ** -0.5, 0.25)
    up_bias = normal_values(key_of[8], (FF,), 0.3, 1.5, (), jnp.float32)
    down_weight = normal_values(key_of[9], (FF, D), (FF // 2) ** -0.5, 0.1875)
    down_bias = normal_values(key_of[10], (D,), 0.3, 1.5, (), jnp.float32)
    head_weight = normal_values(key_of[11], (D, 6), 0.1, 0.59765625)
    species = plant(ranked_ids(key_of[12], (WINDOWS,), SPECIES, 2), jax.random.fold_in(key_of[12], 3), 0, SPECIES - 1).astype(jnp.int32)
    cotangent = normal_values(key_of[13], (WINDOWS, WINDOW_BASES, D), 1.0, 6.0, ((0, 16), (1, 2)))
    return {"inputs": inputs, "conv_weight": conv_weight, "conv_bias": conv_bias, "norm1_gain": norm1_gain, "norm1_shift": norm1_shift, "norm2_gain": norm2_gain, "norm2_shift": norm2_shift, "up_weight": up_weight, "up_bias": up_bias, "down_weight": down_weight, "down_bias": down_bias, "head_weight": head_weight, "species": species, "cotangent": cotangent}


EPS = 1e-05

@jax.custom_vjp
def low(v):
    return lax.optimization_barrier(v.astype(jnp.bfloat16)).astype(jnp.float32)

@jax.custom_vjp
def low_back(v):
    return v

def low_keep(v):
    return (low(v), None)

def low_pass(kept, grad):
    return (grad,)

def back_keep(v):
    return (v, None)

def back_low(kept, grad):
    return (low(grad),)
low.defvjp(low_keep, low_pass)
low_back.defvjp(back_keep, back_low)

def norm_rows(value, gain, shift):
    centre = value - lax.optimization_barrier(jnp.mean(value, axis=-1, keepdims=True))
    spread = lax.optimization_barrier(jnp.mean(centre * centre, axis=-1, keepdims=True))
    return centre * lax.rsqrt(spread + EPS) * gain + shift

def smooth(value):
    return jax.nn.gelu(value, approximate=False)

def conv_rows(normed, conv_weight, conv_bias):
    padded_input = jnp.pad(normed, ((0, 0), (RIM, RIM), (0, 0)))
    total = conv_bias
    for kernel_offset in range(KER):
        window_slice = padded_input[:, kernel_offset * DILATION_STEP:kernel_offset * DILATION_STEP + WINDOW_BASES]
        total = total + jnp.einsum('btd,de->bte', window_slice, conv_weight[kernel_offset], precision=lax.Precision.HIGHEST)
    return total

def block(x, conv_weight, conv_bias, norm1_gain, norm1_shift, norm2_gain, norm2_shift, up_weight, up_bias, down_weight, down_bias):
    normed = low(norm_rows(x, norm1_gain, norm1_shift))
    mixed = low_back(conv_rows(normed, conv_weight, conv_bias))
    hidden = x + smooth(mixed)
    second = low(norm_rows(hidden, norm2_gain, norm2_shift))
    inner = low_back(jnp.einsum('btd,df->btf', second, up_weight, precision=lax.Precision.HIGHEST) + up_bias)
    active = low(smooth(inner))
    return hidden + jnp.einsum('btf,fd->btd', active, down_weight, precision=lax.Precision.HIGHEST) + down_bias

def reference(inputs, conv_weight, conv_bias, norm1_gain, norm1_shift, norm2_gain, norm2_shift, up_weight, up_bias, down_weight, down_bias, head_weight, species, cotangent):
    params = (conv_weight.astype(jnp.float32), conv_bias, norm1_gain, norm1_shift, norm2_gain, norm2_shift, up_weight.astype(jnp.float32), up_bias, down_weight.astype(jnp.float32), down_bias)
    groups = WINDOWS // WIN_DEV
    grouped_in = inputs.reshape(groups, WIN_DEV, WINDOW_BASES, D)
    grouped_co = cotangent.reshape(groups, WIN_DEV, WINDOW_BASES, D)

    def step(carry, item):
        part_in, part_co = item
        output, pull = jax.vjp(block, part_in.astype(jnp.float32), *params)
        grads = pull(part_co.astype(jnp.float32))
        carry = tuple((c + g for c, g in zip(carry, grads[1:])))
        return (carry, (output.astype(jnp.bfloat16), grads[0].astype(jnp.bfloat16)))
    start = tuple((jnp.zeros(p.shape, jnp.float32) for p in params))
    totals, (outputs, in_grads) = lax.scan(step, start, (grouped_in, grouped_co))
    activations = outputs.reshape(WINDOWS, WINDOW_BASES, D)
    input_grad = in_grads.reshape(WINDOWS, WINDOW_BASES, D)
    logits = jnp.dot(activations.reshape(WINDOWS * WINDOW_BASES, D), head_weight, preferred_element_type=jnp.float32)
    probs = jax.nn.softmax(logits, axis=-1)
    window_sums = lax.optimization_barrier(jnp.sum(probs.reshape(WINDOWS, WINDOW_BASES, 6), axis=1))
    onehot = (species[:, None] == jnp.arange(SPECIES, dtype=jnp.int32)[None, :]).astype(jnp.float32)
    frequencies = jnp.dot(onehot.T, window_sums, precision=lax.Precision.HIGHEST) / WINDOW_BASES
    return (activations, input_grad, totals[0], totals[1], totals[2], totals[3], totals[4], totals[5], totals[6], totals[7], totals[8], totals[9], frequencies)
```

```python
import functools

import jax
import jax.numpy as jnp
from jax import lax
from jax.experimental import pallas as pl
from jax.experimental.pallas import tpu as pltpu
from jax.sharding import PartitionSpec as P

DILATION_STEP = 8
WINDOW_BASES = 512
SPECIES = 8
EPS = 1e-05
MB = 1 << 20
f32 = jnp.float32
bf16 = jnp.bfloat16

ERFC_SCALE = 0.38
ERFC_TERMS = (
    0.2143115242181569,
    0.2163001978168039,
    0.18185270480262436,
    0.24492249564934945,
    -0.06627411566118212,
    0.33369741119693175,
    -0.12481121287693218,
)


def normal_parts(u):
    t = 1.0 / (1.0 + (ERFC_SCALE * 0.5**0.5) * jnp.abs(u))
    series = jnp.full_like(t, 0.5 * ERFC_TERMS[-1])
    for term in ERFC_TERMS[-2::-1]:
        series = series * t + 0.5 * term
    bell = jnp.exp(-0.5 * (u * u))
    tail = series * t * bell
    return jnp.where(u < 0, tail, 1.0 - tail), u * (bell * 0.3989422804014327)


def centred(value):
    centre = value - jnp.mean(value, axis=-1, keepdims=True)
    scale = lax.rsqrt(jnp.mean(centre * centre, axis=-1, keepdims=True) + EPS)
    return centre * scale, scale


def contract(a, b, dim_a, dim_b):
    return lax.dot_general(a, b, (((dim_a,), (dim_b,)), ((), ())), preferred_element_type=f32)


def spec_whole(shape):
    return pl.BlockSpec(shape, lambda i, *_: (0,) * len(shape))


def spec_window(shape):
    return pl.BlockSpec((1,) + shape[1:], lambda i, *_: (i, 0, 0))


def shape_of(shape, dtype):
    return jax.ShapeDtypeStruct(shape, dtype)


def fill_window(pad, both, core, rim, own, other):
    seg = own.shape[0]
    extent = 2 * seg + 2 * rim
    zeros = jnp.zeros((rim, own.shape[1]), f32)
    pad[0:rim, :] = zeros
    pad[extent - rim : extent, :] = zeros
    pad[pl.ds(pl.multiple_of(rim + core * seg, 16), seg), :] = own
    pad[pl.ds(pl.multiple_of(rim + (1 - core) * seg, 16), seg), :] = other
    both[0] = pad[...].astype(bf16)
    both[1, 0 : extent - 16, :] = pad[8 : extent - 8, :].astype(bf16)


def conv_kernel(rim, core_ref, x_ref, xp_ref, w_ref, b_ref, g1_ref, s1_ref, g2_ref, s2_ref, a_ref, h_ref, gp_ref, n_ref, pad, both):
    seg = x_ref.shape[1]
    core = core_ref[0]
    x = x_ref[0].astype(f32)
    g1, s1 = g1_ref[...], s1_ref[...]
    own = centred(x)[0] * g1 + s1
    other = centred(xp_ref[0].astype(f32))[0] * g1 + s1
    fill_window(pad, both, core, rim, own, other)
    a_ref[0] = both[0, rim : rim + 2 * seg, :]
    u = b_ref[...]
    for k in range(w_ref.shape[0]):
        start = pl.multiple_of(core * seg + (k - k % 2) * DILATION_STEP, 16)
        u = u + jnp.dot(both[k % 2, pl.ds(start, seg), :], w_ref[k], preferred_element_type=f32)
    cdf, slope = normal_parts(u)
    h = x + u * cdf
    gp_ref[0] = cdf + slope
    h_ref[0] = h
    n_ref[0] = (centred(h)[0] * g2_ref[...] + s2_ref[...]).astype(bf16)


def conv_forward(core, x, xp, w, b, g1, s1, g2, s2):
    nw, seg, d = x.shape
    rim = (w.shape[0] - 1) // 2 * DILATION_STEP
    outs = ((nw, 2 * seg, d), bf16), ((nw, seg, d), f32), ((nw, seg, d), f32), ((nw, seg, d), bf16)
    return pl.pallas_call(
        functools.partial(conv_kernel, rim),
        out_shape=tuple(shape_of(*o) for o in outs),
        grid_spec=pltpu.PrefetchScalarGridSpec(
            num_scalar_prefetch=1,
            grid=(nw,),
            in_specs=[spec_window(x.shape), spec_window(x.shape), spec_whole(w.shape)] + [spec_whole((1, d))] * 5,
            out_specs=[spec_window(o[0]) for o in outs],
            scratch_shapes=[
                pltpu.VMEM((2 * seg + 2 * rim, d), f32),
                pltpu.VMEM((2, 2 * seg + 2 * rim, d), bf16),
            ],
        ),
        compiler_params=pltpu.CompilerParams(vmem_limit_bytes=30 * MB),
        name="conv_forward",
    )(core, x, xp, w, *(v.reshape(1, d) for v in (b, g1, s1, g2, s2)))


FF_BLOCK = 512
ROWS = 256
COLS = 256


def ffn_kernel(first, core_ref, n_ref, dy_ref, up_ref, ub_ref, down_ref, *refs):
    if first:
        send_ref, keep_ref, ubg_ref, out_ref, dn_ref, q_s, dz_s = refs
    else:
        (out_in, dn_in, h_ref, gp_ref, db_ref, g2_ref, send_ref, keep_ref, ubg_ref, act_ref, dh_ref, du_ref, sums_ref, out_ref, dn_ref, q_s, dz_s) = refs
    core = core_ref[0]
    rows = n_ref.shape[0]
    chunks = rows // ROWS
    parts = FF_BLOCK // COLS

    def column(block):
        return pl.multiple_of((core if block else 1 - core) * FF_BLOCK, FF_BLOCK)

    def early(block, unit):
        part, chunk = unit // chunks, unit % chunks
        r = slice(chunk * ROWS, (chunk + 1) * ROWS)
        c = pl.ds(pl.multiple_of(column(block) + part * COLS, COLS), COLS)
        z = jnp.dot(n_ref[r, :], up_ref[:, c], preferred_element_type=f32) + ub_ref[:, c]
        dq = contract(dy_ref[r, :], down_ref[c, :], 1, 1)
        cdf, slope = normal_parts(z)
        here = slice(part * COLS, (part + 1) * COLS)
        q_s[block, r, here] = (z * cdf).astype(bf16)
        dz = dq * (cdf + slope)
        dz_s[block, r, here] = dz.astype(bf16)
        return jnp.sum(dz, axis=0, keepdims=True)

    def rows_late(block, chunk):
        r = slice(chunk * ROWS, (chunk + 1) * ROWS)
        c = pl.ds(column(block), FF_BLOCK)
        out = jnp.dot(q_s[block, r, :], down_ref[c, :], preferred_element_type=f32)
        dn = contract(dz_s[block, r, :], up_ref[:, c], 1, 1)
        if first and block == 0:
            out_ref[r, :] = out
            dn_ref[r, :] = dn
        elif block == 0:
            out_ref[r, :] = out_in[r, :] + out
            dn_ref[r, :] = dn_in[r, :] + dn
        else:
            out_ref[r, :] += out
            dn_ref[r, :] += dn

    def weights_late(block, piece):
        target = keep_ref if block else send_ref
        half = FF_BLOCK // 2
        if piece < 2:
            g = contract(q_s[block, :, piece * half : (piece + 1) * half], dy_ref[...], 0, 0)
            target[piece * 2 * half : piece * 2 * half + half, :] = g.astype(bf16)
        else:
            piece -= 2
            g = contract(n_ref[:, piece * half : (piece + 1) * half], dz_s[block], 0, 0)
            target[piece * 2 * half + half : (piece + 1) * 2 * half, :] = g.astype(bf16)

    def late(block, unit):
        if unit < chunks:
            rows_late(block, unit)
        elif unit < chunks + 4:
            weights_late(block, unit - chunks)

    units = parts * chunks
    assert chunks + 4 <= units
    for block in range(2):
        total = [None] * parts
        for unit in range(units):
            s = early(block, unit)
            part = unit // chunks
            total[part] = s if total[part] is None else total[part] + s
            if block:
                late(0, unit)
        for part in range(parts):
            ubg_ref[:, pl.ds(pl.multiple_of(column(block) + part * COLS, COLS), COLS)] = total[part]
    for chunk in range(chunks):
        rows_late(1, chunk)
    if first:
        for piece in range(4):
            weights_late(1, piece)
        return
    g2 = g2_ref[...]
    sums = [None] * 4
    for chunk in range(chunks):
        r = slice(chunk * ROWS, (chunk + 1) * ROWS)
        h = h_ref[r, :]
        dy = dy_ref[r, :].astype(f32)
        act_ref[r, :] = (h + out_ref[r, :] + db_ref[...]).astype(bf16)
        hat, scale = centred(h)
        dn = dn_ref[r, :]
        dhat = dn * g2
        dh = dy + scale * (
            dhat - jnp.mean(dhat, axis=-1, keepdims=True) - hat * jnp.mean(dhat * hat, axis=-1, keepdims=True)
        )
        dh_ref[r, :] = dh
        du = dh * gp_ref[r, :]
        du_ref[r, :] = du.astype(bf16)
        for i, v in enumerate((du, dn * hat, dn, dy)):
            s = jnp.sum(v, axis=0, keepdims=True)
            sums[i] = s if sums[i] is None else sums[i] + s
        weights_late(1, chunk) if chunk < 4 else None
    for piece in range(chunks, 4):
        weights_late(1, piece)
    for i in range(4):
        sums_ref[i : i + 1, :] = sums[i]


def ffn(first, group, core, n, dy, up, ub, down, extra=()):
    rows, d = n.shape
    span = 2 * FF_BLOCK
    grads = ((2 * FF_BLOCK, d), bf16), ((2 * FF_BLOCK, d), bf16), ((1, span), f32)
    acc = ((rows, d), f32), ((rows, d), f32)
    if first:
        outs = grads + acc
        scratch = []
    else:
        outs = grads + (((rows, d), bf16), ((rows, d), f32), ((rows, d), bf16), ((4, d), f32))
        scratch = [pltpu.VMEM((rows, d), f32)] * 2
    return pl.pallas_call(
        functools.partial(ffn_kernel, first),
        out_shape=tuple(shape_of(*o) for o in outs),
        grid_spec=pltpu.PrefetchScalarGridSpec(
            num_scalar_prefetch=1,
            grid=(1,),
            in_specs=[
                spec_whole(n.shape),
                spec_whole(dy.shape),
                pl.BlockSpec((d, span), lambda i, *_: (0, group)),
                pl.BlockSpec((1, span), lambda i, *_: (0, group)),
                pl.BlockSpec((span, d), lambda i, *_: (group, 0)),
            ]
            + [spec_whole(e.shape) for e in extra],
            out_specs=[spec_whole(o[0]) for o in outs],
            scratch_shapes=scratch + [pltpu.VMEM((2, rows, FF_BLOCK), bf16)] * 2,
        ),
        compiler_params=pltpu.CompilerParams(vmem_limit_bytes=50 * MB),
        name="ffn_first" if first else "ffn_second",
    )(core, n, dy, up, ub.reshape(1, -1), down, *extra)


def conv_weight_kernel(rim, core_ref, part_ref, a_ref, du_ref, dup_ref, out_ref, pad, both):
    core, part = core_ref[0], part_ref[0]
    nw, seg, d = du_ref.shape
    half = d // 2
    extent = 2 * seg + 2 * rim
    cols = pl.ds(pl.multiple_of(core * half, half), half)
    for w in range(nw):
        zeros = jnp.zeros((rim, half), f32)
        pad[w, 0:rim, :] = zeros
        pad[w, extent - rim : extent, :] = zeros
        pad[w, pl.ds(pl.multiple_of(rim + core * seg, 16), seg), :] = du_ref[w, :, cols].astype(f32)
        pad[w, pl.ds(pl.multiple_of(rim + (1 - core) * seg, 16), seg), :] = dup_ref[w, :, cols].astype(f32)
        both[0, w] = pad[w].astype(bf16)
        both[1, w, 0 : extent - 16, :] = pad[w, 8 : extent - 8, :].astype(bf16)
    blocks = out_ref.shape[0] // half
    for i in range(blocks):
        block = part * blocks + i
        tap = block // 2
        odd = lax.rem(tap, 2)
        lanes = pl.ds(pl.multiple_of(lax.rem(block, 2) * half, half), half)
        start = pl.multiple_of(2 * rim - (tap + odd) * DILATION_STEP, 16)
        right = both[odd, :, pl.ds(start, 2 * seg), :].reshape(nw * 2 * seg, half)
        left = a_ref[:, :, lanes].reshape(nw * 2 * seg, half)
        out_ref[i * half : (i + 1) * half, :] = contract(left, right, 0, 0).astype(bf16)


def conv_weight(core, part, a, du, dup, taps):
    nw, seg, d = du.shape
    rim = (taps - 1) // 2 * DILATION_STEP
    extent = 2 * seg + 2 * rim
    out = (taps * d // 2, d // 2)
    return pl.pallas_call(
        functools.partial(conv_weight_kernel, rim),
        out_shape=shape_of(out, bf16),
        grid_spec=pltpu.PrefetchScalarGridSpec(
            num_scalar_prefetch=2,
            grid=(1,),
            in_specs=[spec_whole(a.shape), spec_whole(du.shape), spec_whole(du.shape)],
            out_specs=spec_whole(out),
            scratch_shapes=[pltpu.VMEM((nw, extent, d // 2), f32), pltpu.VMEM((2, nw, extent, d // 2), bf16)],
        ),
        compiler_params=pltpu.CompilerParams(vmem_limit_bytes=40 * MB),
        name="conv_weight",
    )(core, part, a, du, dup)


def conv_input_kernel(rim, core_ref, du_ref, dup_ref, w_ref, dh_ref, x_ref, g1_ref, grad_ref, sums_ref, pad, both):
    seg = x_ref.shape[1]
    core = core_ref[0]
    fill_window(pad, both, core, rim, du_ref[0].astype(f32), dup_ref[0].astype(f32))
    da = None
    for k in range(w_ref.shape[0]):
        start = pl.multiple_of(core * seg + 2 * rim - (k + k % 2) * DILATION_STEP, 16)
        v = contract(both[k % 2, pl.ds(start, seg), :], w_ref[k], 1, 1)
        da = v if da is None else da + v
    hat, scale = centred(x_ref[0].astype(f32))
    dhat = da * g1_ref[...]
    back = scale * (dhat - jnp.mean(dhat, axis=-1, keepdims=True) - hat * jnp.mean(dhat * hat, axis=-1, keepdims=True))
    grad_ref[0] = (dh_ref[0] + back).astype(bf16)

    @pl.when(pl.program_id(0) == 0)
    def _():
        sums_ref[...] = jnp.zeros_like(sums_ref)

    sums_ref[0:1, :] += jnp.sum(da * hat, axis=0, keepdims=True)
    sums_ref[1:2, :] += jnp.sum(da, axis=0, keepdims=True)


def conv_input(core, du, dup, w, dh, x, g1):
    nw, seg, d = x.shape
    rim = (w.shape[0] - 1) // 2 * DILATION_STEP
    return pl.pallas_call(
        functools.partial(conv_input_kernel, rim),
        out_shape=(shape_of(x.shape, bf16), shape_of((2, d), f32)),
        grid_spec=pltpu.PrefetchScalarGridSpec(
            num_scalar_prefetch=1,
            grid=(nw,),
            in_specs=[spec_window(x.shape), spec_window(x.shape), spec_whole(w.shape), spec_window(x.shape), spec_window(x.shape), spec_whole((1, d))],
            out_specs=[spec_window(x.shape), spec_whole((2, d))],
            scratch_shapes=[
                pltpu.VMEM((2 * seg + 2 * rim, d), f32),
                pltpu.VMEM((2, 2 * seg + 2 * rim, d), bf16),
            ],
        ),
        compiler_params=pltpu.CompilerParams(vmem_limit_bytes=30 * MB),
        name="conv_input",
    )(core, du, dup, w, dh, x, g1.reshape(1, d))


def swap_cores(value):
    return lax.ppermute(value, "seq", [(0, 1), (1, 0)])


def exchange(value, bits):
    count = lax.axis_size("batch")
    pairs = [(c * count + i, c * count + (i ^ (1 << bits[c]))) for c in range(2) for i in range(count)]
    return lax.ppermute(value, ("seq", "batch"), pairs)


def own_bit(bits):
    place = lax.axis_index("batch")
    return (place >> jnp.where(lax.axis_index("seq") == 0, bits[0], bits[1])) & 1


ORDER = ((0, 1), (1, 0), (2, 3), (3, 2))


def halves(value, bit):
    h = value.shape[0] // 2
    return lax.dynamic_slice_in_dim(value, bit * h, h, 0), lax.dynamic_slice_in_dim(value, (1 - bit) * h, h, 0)


def joined(own, other, bit):
    return jnp.where(bit == 0, jnp.concatenate([own, other], 0), jnp.concatenate([other, own], 0))


def summed(a, b):
    return (a.astype(f32) + b.astype(f32)).astype(bf16)


def chips_total(keep, send):
    count = lax.axis_size("batch")
    stages = ORDER[: count.bit_length() - 1]
    for i, bits in enumerate(stages):
        held = summed(keep, exchange(send, bits))
        if i + 1 < len(stages):
            keep, send = halves(held, own_bit(stages[i + 1]))
    if count > 1 << len(stages):
        step = 1 << len(stages)
        groups = [[j + step * i for i in range(count // step)] for j in range(step)]
        held = lax.psum(held, "batch", axis_index_groups=groups)
    for bits in stages[:0:-1]:
        held = joined(held, exchange(held, bits), own_bit(bits))
    return held, exchange(held, stages[0])


def body(
    inputs,
    conv_weight_,
    conv_bias,
    norm1_gain,
    norm1_shift,
    norm2_gain,
    norm2_shift,
    up_weight,
    up_bias,
    down_weight,
    down_bias,
    head_weight,
    species,
    cotangent,
):
    nw, seg, d = inputs.shape
    taps = conv_weight_.shape[0]
    ff = up_weight.shape[1]
    rows = nw * seg
    core_i = lax.axis_index("seq")
    core = core_i.astype(jnp.int32).reshape(1)
    dy = cotangent.reshape(rows, d)
    a, h, gp, n = conv_forward(core, inputs, swap_cores(inputs), conv_weight_, conv_bias, norm1_gain, norm1_shift, norm2_gain, norm2_shift)
    h, gp, n = (v.reshape(rows, d) for v in (h, gp, n))
    send1, keep1, ubg1, out, dn = ffn(True, 0, core, n, dy, up_weight, up_bias, down_weight)
    send2, keep2, ubg2, act, dh, du, sums2 = ffn(
        False, 1, core, n, dy, up_weight, up_bias, down_weight,
        (out, dn, h, gp, down_bias.reshape(1, d), norm2_gain.reshape(1, d)),
    )
    du = du.reshape(nw, seg, d)
    dup = swap_cores(du)
    bit0 = own_bit(ORDER[0]).astype(jnp.int32)
    send3 = conv_weight(core, (1 - bit0).reshape(1), a, du, dup, taps)
    keep3 = conv_weight(core, bit0.reshape(1), a, du, dup, taps)
    input_grad, sums1 = conv_input(core, du, dup, conv_weight_, dh.reshape(nw, seg, d), inputs, norm1_gain)

    logits = jnp.dot(act, head_weight, preferred_element_type=f32)
    probs = jax.nn.softmax(logits, axis=-1)
    window_sums = jnp.sum(probs.reshape(nw, seg, -1), axis=1)
    onehot = (species[:, None] == jnp.arange(SPECIES, dtype=jnp.int32)[None, :]).astype(f32)
    freq = jnp.dot(onehot.T, window_sums, precision=lax.Precision.HIGHEST)
    freq_row = jnp.pad(freq.reshape(-1), (0, d - freq.size))
    small = jnp.concatenate(
        [sums2, sums1, freq_row[None], jnp.concatenate([ubg1, ubg2], 1).reshape(-1, d)], axis=0
    )
    count = lax.axis_size("batch")
    small = small + swap_cores(small)
    for b in range(count.bit_length() - 1):
        small = small + exchange(small, (b, b))

    totals = []
    for keep, send in ((keep1, send1), (keep2, send2)):
        held = summed(keep, swap_cores(send))
        totals.append(chips_total(*halves(held, bit0)))
    totals.append(chips_total(keep3, send3))

    def spread(pair):
        own, other = pair
        mine = joined(own, other, bit0)
        theirs = swap_cores(mine)
        return jnp.where(core_i == 0, mine, theirs).astype(f32), jnp.where(core_i == 0, theirs, mine).astype(f32)

    t1, t2, t3 = (spread(t) for t in totals)
    blocks = (t1[0], t1[1], t2[0], t2[1])
    half = FF_BLOCK // 2
    down_grad = jnp.concatenate([p for b in blocks for p in (b[0:half], b[2 * half : 3 * half])], 0)
    up_grad = jnp.concatenate([jnp.concatenate([b[half : 2 * half], b[3 * half : 4 * half]], 0) for b in blocks], 1)
    conv_grad = jnp.concatenate(t3, 1).reshape(taps, d, d)
    frequencies = small[6, : freq.size].reshape(freq.shape) / WINDOW_BASES
    return (
        act.reshape(nw, seg, d),
        input_grad,
        conv_grad,
        small[0],
        small[4],
        small[5],
        small[1],
        small[2],
        up_grad,
        small[7:].reshape(ff),
        down_grad,
        small[3],
        frequencies,
    )


def solution(mesh):
    rows = P("batch", "seq", None)
    placed = (rows,) + (P(),) * 11 + (P("batch"), rows)
    return jax.shard_map(
        body, mesh=mesh, in_specs=placed, out_specs=(rows, rows) + (P(),) * 11, check_vma=False
    )
```

```python
import functools

import jax
import jax.numpy as jnp
from jax import lax
from jax.experimental import pallas as pl
from jax.experimental.pallas import tpu as pltpu
from jax.sharding import PartitionSpec as P

DILATION_STEP = 8
WINDOW_BASES = 512
SPECIES = 8
EPS = 1e-05
MB = 1 << 20
f32 = jnp.float32
bf16 = jnp.bfloat16

IN_VMEM = pl.BlockSpec(memory_space=pltpu.VMEM)
ANYWHERE = pl.BlockSpec(memory_space=pl.ANY)

BIT0, BIT1, BIT2, CORE, OTHER_BIT0 = range(5)

PLANE, ACROSS, NEAR, FAR = (0, 1), (1, 0), (2, 2), (3, 3)
LONG = (
    ("halve", PLANE), ("halve", ACROSS), ("halve", NEAR), ("whole", FAR),
    ("join", NEAR), ("join", ACROSS), ("join", PLANE),
)
SHORT = (
    ("halve", PLANE), ("halve", ACROSS), ("whole", (2, 3)), ("whole", (3, 2)),
    ("join", ACROSS), ("join", PLANE),
)
PLACE_OF = {PLANE: BIT0, ACROSS: BIT1, NEAR: BIT2}


def normal_parts(u):
    return 0.5 + 0.5 * lax.erf(u * 0.5**0.5), u * (jnp.exp(-0.5 * (u * u)) * 0.3989422804014327)


def centred(value):
    centre = value - jnp.mean(value, axis=-1, keepdims=True)
    scale = lax.rsqrt(jnp.mean(centre * centre, axis=-1, keepdims=True) + EPS)
    return centre * scale, scale


def norm_back(grad, hat, scale):
    return scale * (grad - jnp.mean(grad, axis=-1, keepdims=True) - hat * jnp.mean(grad * hat, axis=-1, keepdims=True))


def contract(a, b, dim_a, dim_b):
    return lax.dot_general(a, b, (((dim_a,), (dim_b,)), ((), ())), preferred_element_type=f32)


def column_sum(value):
    return jnp.sum(value, axis=0, keepdims=True)


def added(total, value):
    return value if total is None else total + value


MARK = ((8, 128), f32, "v")


def places_here():
    core = lax.axis_index("seq")
    place = lax.axis_index("batch")

    def bit(bits, at):
        return lax.shift_right_logical(place, bits[0] + at * (bits[1] - bits[0])) & 1

    return bit(PLANE, core), bit(ACROSS, core), bit(NEAR, core), core, bit(PLANE, 1 - core)


class Calls:
    def __init__(self):
        self.last = None
        self.also = []

    def __call__(self, kernel, name, outs, ins, scratch=(), limit=8, aliases=None):
        count = len(ins)
        tokens = self.also + ([] if self.last is None else [self.last])
        self.also = []

        def run(*refs):
            kernel(places_here(), *refs[:count], *refs[count + len(tokens) :])

        places = {"v": pltpu.VMEM, "a": pltpu.HBM}
        values = [pltpu.with_memory_space_constraint(x, places[w]) if w in places else x for x, w in ins]
        result = pl.pallas_call(
            run,
            out_shape=tuple(places[w](s, d) for s, d, w in outs),
            in_specs=[{"v": IN_VMEM, "a": ANYWHERE}[w] for _, w in ins] + [ANYWHERE] * len(tokens),
            out_specs=tuple(IN_VMEM if w == "v" else ANYWHERE for _, _, w in outs),
            scratch_shapes=list(scratch),
            input_output_aliases=aliases or {},
            compiler_params=pltpu.CompilerParams(vmem_limit_bytes=limit * MB),
            cost_estimate=pl.CostEstimate(flops=20*10**9, bytes_accessed=1, transcendentals=0),
            name=name,
        )(*values, *tokens)
        result = tuple(result)
        self.last = min(result, key=lambda x: x.size)
        return result

    def follows(self, value):
        self.also.append(value)


def window_scratch(count, seg, rim, width):
    extent = seg + 2 * rim
    return [pltpu.VMEM((extent, width), f32) for _ in range(count)] + [
        pltpu.VMEM((2, extent, width), bf16) for _ in range(count)
    ]


def fill_segment(pad, both, core, rim, own, other):
    seg = own.shape[0]
    extent = seg + 2 * rim
    pad[0:rim, :] = jnp.where(core == 0, 0.0, other[seg - rim :, :])
    pad[rim : rim + seg, :] = own
    pad[rim + seg :, :] = jnp.where(core == 0, other[0:rim, :], 0.0)
    both[0] = pad[...].astype(bf16)
    both[1, 0 : extent - 16, :] = pad[8 : extent - 8, :].astype(bf16)


def prepare_kernel(rim, s, x_any, w_any, *refs):
    vec_anys, (a_ref, both_ref, w_ref, x_ref, vec_ref, pad, sems) = refs[:6], refs[6:]
    nw, seg, d = x_ref.shape
    extent = seg + 2 * rim
    core = s[CORE]
    copies = [pltpu.make_async_copy(v, vec_ref.at[i : i + 1], sems.at[i]) for i, v in enumerate(vec_anys)]
    copies += [pltpu.make_async_copy(x_any.at[i], x_ref.at[i], sems.at[6 + i]) for i in range(nw)]
    weights = [pltpu.make_async_copy(w_any.at[k], w_ref.at[k], sems.at[6 + nw + k]) for k in range(w_ref.shape[0])]
    for copy in copies + weights:
        copy.start()
    for copy in copies[:6]:
        copy.wait()
    for w in range(nw):
        copies[6 + w].wait()
        own = centred(x_ref[w].astype(f32))[0] * vec_ref[1:2, :] + vec_ref[2:3, :]
        pad[w, rim : rim + seg, :] = own
        own = own.astype(bf16)
        a_ref[w, pl.ds(pl.multiple_of(core * seg, seg), seg), :] = own
        both_ref[0, w, rim : rim + seg, :] = own
        both_ref[1, w, rim : rim + seg - 16, :] = pad[w, rim + 8 : rim + seg - 8, :].astype(bf16)
    for copy in weights:
        copy.wait()


def set_rims(both_ref, w, core, rim, seg, near_left, near_right):
    left = jnp.where(core == 0, 0.0, near_left)
    right = jnp.where(core == 0, near_right, 0.0)
    end = rim + seg
    both_ref[0, w, 0:rim, :] = left.astype(bf16)
    both_ref[0, w, end : end + rim, :] = right.astype(bf16)
    first = both_ref[0, w, rim : rim + 16, :].astype(f32)[0:8]
    last = both_ref[0, w, end - 16 : end, :].astype(f32)[8:16]
    both_ref[1, w, 0:rim, :] = jnp.concatenate([left[8:], first], axis=0).astype(bf16)
    both_ref[1, w, end - 16 : end + rim - 16, :] = jnp.concatenate([last, right[: rim - 8]], axis=0).astype(bf16)


def conv_kernel(rim, s, xp_ref, both_in, w_ref, x_ref, vec_ref, dy_any, up_any, down_any, h_ref, gp_ref, n_ref, dy_ref, up_ref, down_ref, both_ref, sems):
    nw, seg, _ = x_ref.shape
    taps = w_ref.shape[0]
    core = s[CORE]
    copies = [
        pltpu.make_async_copy(a, b, sems.at[i])
        for i, (a, b) in enumerate(((dy_any, dy_ref), (up_any, up_ref), (down_any, down_ref)))
    ]
    for copy in copies:
        copy.start()
    bias, g1, s1, g2, s2 = (vec_ref[i : i + 1, :] for i in range(5))

    def rims(w):
        near_left = centred(xp_ref[w, seg - rim :, :].astype(f32))[0] * g1 + s1
        near_right = centred(xp_ref[w, 0:rim, :].astype(f32))[0] * g1 + s1
        set_rims(both_ref, w, core, rim, seg, near_left, near_right)

    def finish(w, u):
        x = x_ref[w].astype(f32)
        cdf, slope = normal_parts(u)
        h = x + u * cdf
        gp_ref[w] = cdf + slope
        h_ref[w] = h
        n_ref[w] = (centred(h)[0] * g2 + s2).astype(bf16)

    for w in range(nw):
        rims(w)
    before = None
    for w in range(nw):
        u = bias
        for k in range(taps):
            start = (k - k % 2) * DILATION_STEP
            u = u + jnp.dot(both_ref[k % 2, w, start : start + seg, :], w_ref[k], preferred_element_type=f32)
            if k == 4 and before is not None:
                finish(w - 1, before)
        before = u
    finish(nw - 1, before)
    for copy in copies:
        copy.wait()


FF_BLOCK = 512
CHUNK = 256
COLS = 256
HALF = FF_BLOCK // 2


def block_column(number, core):
    return pl.multiple_of(((number % 2) * 2 + (core if number >= 2 else 1 - core)) * FF_BLOCK, FF_BLOCK)


def ffn_kernel(index, s, n_ref, dy_ref, up_ref, ub_ref, down_ref, *refs):
    keeps = index >= 2
    if keeps:
        recv_ref, ubg_in, keep_ref, send_ref, q_s, dz_s, ubg_ref, part_s = refs
    elif index:
        ubg_in, send_ref, q_s, dz_s, ubg_ref, part_s = refs
    else:
        send_ref, q_s, dz_s, ubg_ref, part_s = refs
    rows = n_ref.shape[0]
    chunks = rows // CHUNK
    parts = FF_BLOCK // COLS
    column = block_column(index, s[CORE])
    total = [None] * parts

    def early(chunk, part):
        r = slice(chunk * CHUNK, (chunk + 1) * CHUNK)
        c = pl.ds(pl.multiple_of(column + part * COLS, COLS), COLS)
        z = jnp.dot(n_ref[r, :], up_ref[:, c], preferred_element_type=f32) + ub_ref[:, c]
        dq = contract(dy_ref[r, :], down_ref[c, :], 1, 1)
        cdf, slope = normal_parts(z)
        here = slice(part * COLS, (part + 1) * COLS)
        q_s[r, here] = (z * cdf).astype(bf16)
        dz = dq * (cdf + slope)
        dz_s[r, here] = dz.astype(bf16)
        total[part] = added(total[part], column_sum(dz))

    def weights(stage, piece):
        kept, of_up = piece // 2, piece % 2
        half = (s[BIT0] if kept else 1 - s[BIT0]) if keeps else kept
        lanes = pl.ds(pl.multiple_of(half * HALF, HALF), HALF)
        r = slice(stage * rows // 2, (stage + 1) * rows // 2)
        if of_up:
            g = contract(n_ref[r, lanes], dz_s[r, :], 0, 0)
        else:
            g = contract(q_s[r, lanes], dy_ref[r, :], 0, 0)
        place = slice(piece * HALF, (piece + 1) * HALF)
        if stage == 0:
            part_s[place, :] = g
            return
        g = g + part_s[place, :]
        if not keeps:
            send_ref[place, :] = g.astype(bf16)
            return
        g = g + recv_ref[pl.ds(pl.multiple_of((half * 2 + of_up) * HALF, HALF), HALF), :].astype(f32)
        (keep_ref if kept else send_ref)[of_up * HALF : (of_up + 1) * HALF, :] = g.astype(bf16)

    queue = []
    for chunk in range(chunks):
        for part in range(parts):
            early(chunk, part)
            if queue:
                queue.pop(0)()
        if chunk == chunks // 2 - 1:
            queue += [functools.partial(weights, 0, p) for p in range(4)]
    for p in range(4):
        weights(1, p)
    ubg_ref[...] = ubg_in[...] if index else jnp.zeros_like(ubg_ref)
    for part in range(parts):
        ubg_ref[:, pl.ds(pl.multiple_of(column + part * COLS, COLS), COLS)] = total[part]


def rows_kernel(half, s, dy_ref, up_ref, down_ref, h_ref, gp_ref, vec_ref, *refs):
    q_refs, dz_refs, refs = refs[:4], refs[4:8], refs[8:]
    if half:
        act_in, dh_in, du_in, sums_in, *refs = refs
    else:
        xp_ref, a_in, *refs, a_ref = refs
    act_ref, dh_ref, du_ref, sums_ref = refs
    core = s[CORE]
    rows = dy_ref.shape[0]
    sums = [None] * 4

    def norm_other(w):
        seg = xp_ref.shape[1]
        other = centred(xp_ref[w].astype(f32))[0] * vec_ref[1:2, :] + vec_ref[2:3, :]
        a_ref[w, pl.ds(pl.multiple_of((1 - core) * seg, seg), seg), :] = other.astype(bf16)

    def products(r):
        out = dn = None
        for number in range(4):
            c = pl.ds(block_column(number, core), FF_BLOCK)
            out = added(out, jnp.dot(q_refs[number][r, :], down_ref[c, :], preferred_element_type=f32))
            dn = added(dn, contract(dz_refs[number][r, :], up_ref[:, c], 1, 1))
        return out, dn

    def finish(r, out, dn):
        h = h_ref[r, :]
        dy = dy_ref[r, :].astype(f32)
        act_ref[r, :] = (h + out + vec_ref[5:6, :]).astype(bf16)
        hat, scale = centred(h)
        dh = dy + norm_back(dn * vec_ref[3:4, :], hat, scale)
        dh_ref[r, :] = dh
        du = dh * gp_ref[r, :]
        du_ref[r, :] = du.astype(bf16)
        for i, v in enumerate((du, dn * hat, dn, dy)):
            sums[i] = added(sums[i], column_sum(v))

    before = None
    for chunk in range(half * rows // CHUNK // 2, (half + 1) * rows // CHUNK // 2):
        r = slice(chunk * CHUNK, (chunk + 1) * CHUNK)
        now = products(r)
        if not half:
            for w in range(chunk * 2, chunk * 2 + 2):
                norm_other(w)
        if before is not None:
            finish(*before)
        before = (r, *now)
    finish(*before)
    for i in range(4):
        sums_ref[i : i + 1, :] = sums_in[i : i + 1, :] + sums[i] if half else sums[i]


def conv_weight_kernel(rim, first_block, blocks, kept, fills, s, a_ref, du_ref, dup_ref, *refs):
    if fills:
        out_ref, both, *pads = refs
    else:
        both, out_ref = refs
    core = s[CORE]
    nw, seg, d = du_ref.shape
    half = d // 2
    extent = 2 * seg + 2 * rim
    cols = pl.ds(pl.multiple_of(core * half, half), half)
    if fills:
        for w in range(nw):
            pad = pads[w]
            zeros = jnp.zeros((rim, half), f32)
            pad[0:rim, :] = zeros
            pad[extent - rim : extent, :] = zeros
            pad[pl.ds(pl.multiple_of(rim + core * seg, 16), seg), :] = du_ref[w, :, cols].astype(f32)
            pad[pl.ds(pl.multiple_of(rim + (1 - core) * seg, 16), seg), :] = dup_ref[w, :, cols].astype(f32)
            both[0, w] = pad[...].astype(bf16)
            both[1, w, 0 : extent - 16, :] = pad[8 : extent - 8, :].astype(bf16)
    part = s[BIT0] if kept else 1 - s[BIT0]
    for i in range(blocks):
        block = first_block + part * blocks + i
        tap = block // 2
        odd = lax.rem(tap, 2)
        lanes = pl.ds(pl.multiple_of(lax.rem(block, 2) * half, half), half)
        start = pl.multiple_of(2 * rim - (tap + odd) * DILATION_STEP, 16)
        right = both[odd, :, pl.ds(start, 2 * seg), :].reshape(nw * 2 * seg, half)
        left = a_ref[:, :, lanes].reshape(nw * 2 * seg, half)
        out_ref[i * half : (i + 1) * half, :] = contract(left, right, 0, 0).astype(bf16)


def conv_input_kernel(rim, windows, s, du_ref, dup_ref, w_ref, dh_ref, x_ref, vec_ref, *refs):
    if windows[0]:
        grad_in, sums_in, grad_any, sums_ref, grad, sem, *scratch = refs
    else:
        grad_any, sums_ref, w_out, grad, sem, *scratch = refs
        loads = [pltpu.make_async_copy(w_ref.at[k], w_out.at[k], sem.at[2 + k]) for k in range(w_out.shape[0])]
        for load in loads:
            load.start()
        w_ref = w_out
    seg = x_ref.shape[1]
    core = s[CORE]
    count = len(windows)
    pads, boths = scratch[:count], scratch[count:]
    totals = [None, None]
    copies = []

    def prepare(i):
        fill_segment(pads[i], boths[i], core, rim, du_ref[windows[i]].astype(f32), dup_ref[windows[i]].astype(f32))

    def finish(i, da):
        w = windows[i]
        hat, scale = centred(x_ref[w].astype(f32))
        grad[i] = (dh_ref[w] + norm_back(da * vec_ref[1:2, :], hat, scale)).astype(bf16)
        copies.append(pltpu.make_async_copy(grad.at[i], grad_any.at[w], sem.at[i]))
        copies[-1].start()
        totals[0] = added(totals[0], column_sum(da * hat))
        totals[1] = added(totals[1], column_sum(da))

    prepare(0)
    before = None
    for i in range(count):
        da = None
        for k in range(w_ref.shape[0]):
            if i == 0 and not windows[0]:
                loads[k].wait()
            start = 2 * rim - (k + k % 2) * DILATION_STEP
            da = added(da, contract(boths[i][k % 2, start : start + seg, :], w_ref[k], 1, 1))
            if k == 2 and i + 1 < count:
                prepare(i + 1)
            if k == 5 and before is not None:
                finish(i - 1, before)
        before = da
    finish(count - 1, before)
    for i in range(2):
        sums_ref[i : i + 1, :] = totals[i] + sums_in[i : i + 1, :] if windows[0] else totals[i]
    for copy in copies:
        copy.wait()


SMALL_ROWS = 32


def head_kernel(s, act_ref, head_ref, species_ref, act_any, freq_ref, sem, head_s):
    copy = pltpu.make_async_copy(act_ref, act_any, sem.at[0])
    copy.start()
    classes = head_ref.shape[0]
    head_s[...] = jnp.zeros_like(head_s)
    head_s[0:classes, :] = head_ref[...]
    nw = species_ref.shape[1]
    logits = contract(act_ref[...], head_s[...], 1, 1)
    lane = lax.broadcasted_iota(jnp.int32, logits.shape, 1)
    logits = jnp.where(lane < classes, logits, -jnp.inf)
    e = jnp.exp(logits - jnp.max(logits, axis=-1, keepdims=True))
    probs = e / jnp.sum(e, axis=-1, keepdims=True)
    seg = logits.shape[0] // nw
    row = lax.broadcasted_iota(jnp.int32, freq_ref.shape, 0)
    freq = jnp.zeros(freq_ref.shape, f32)
    for w in range(nw):
        freq = freq + jnp.where(row == species_ref[0:1, w : w + 1], column_sum(probs[w * seg : (w + 1) * seg, :]), 0.0)
    freq_ref[...] = freq
    copy.wait()


def small_kernel(s, sums2_ref, sums1_ref, ubg_ref, freq_ref, out_ref):
    out_ref[...] = jnp.zeros_like(out_ref)
    vectors = [sums2_ref[i : i + 1, :] for i in range(4)] + [sums1_ref[i : i + 1, :] for i in range(2)]
    vectors += [ubg_ref[:, i * 512 : (i + 1) * 512] for i in range(ubg_ref.shape[1] // 512)]
    width = out_ref.shape[1]
    for i, v in enumerate(vectors):
        for j in range(2):
            out_ref[2 * i + j : 2 * i + j + 1, :] = v[:, j * width : (j + 1) * width]
    out_ref[2 * len(vectors) : 2 * len(vectors) + SPECIES, 0 : freq_ref.shape[1]] = freq_ref[...]


def swap_cores(value):
    return lax.ppermute(value, "seq", [(0, 1), (1, 0)])


def exchange(value, bits):
    count = lax.axis_size("batch")
    pairs = [(c * count + i, c * count + (i ^ (1 << bits[c]))) for c in range(2) for i in range(count)]
    return lax.ppermute(value, ("seq", "batch"), pairs)


def add16(a, b):
    return (a.astype(f32) + b.astype(f32)).astype(bf16)


def split_kernel(bit, s, *refs):
    if len(refs) == 4:
        keep_ref, recv_ref, keep_out, send_out = refs
        h = keep_out.shape[0]
        for out, half in ((send_out, 1 - s[bit]), (keep_out, s[bit])):
            r = pl.ds(pl.multiple_of(half * h, 16), h)
            out[...] = add16(keep_ref[r, :], recv_ref[r, :])
        return
    *pairs, keep_out, send_out, whole = refs
    at = 0
    for keep_ref, recv_ref in zip(pairs[::2], pairs[1::2]):
        rows = keep_ref.shape[0]
        whole[at : at + rows, :] = add16(keep_ref[...], recv_ref[...])
        at += rows
    h = keep_out.shape[0]
    for out, half in ((send_out, 1 - s[bit]), (keep_out, s[bit])):
        out[...] = whole[pl.ds(pl.multiple_of(half * h, 16), h), :]


def sum_kernel(s, keep_ref, recv_ref, *refs):
    out_ref = refs[-1]
    h = keep_ref.shape[0]
    out_ref[0:h, :] = add16(keep_ref[...], recv_ref[...])
    if len(refs) == 2:
        out_ref[h:, :] = refs[0][...].astype(bf16)


def join_kernel(h, bit, s, own_ref, recv_ref, out_ref):
    for ref, half in ((own_ref, s[bit]), (recv_ref, 1 - s[bit])):
        out_ref[pl.ds(pl.multiple_of(half * h, 16), h), :] = ref[0:h, :]
    if out_ref.shape[0] > 2 * h:
        out_ref[2 * h :, :] = add16(own_ref[h:, :], recv_ref[h:, :])


def pieces_of(s, refs):
    core = s[CORE]
    places = (s[BIT0], core), (1 - s[BIT0], core), (s[OTHER_BIT0], 1 - core), (1 - s[OTHER_BIT0], 1 - core)
    return [(r, h, c) for r, (h, c) in zip(refs, places)]


def final_ffn_kernel(group, start, s, *refs):
    down_any, up_any, mark, stage, sems = refs[-5:]
    mark[...] = jnp.zeros_like(mark)
    copies = []
    for i, (ref, half, core) in enumerate(pieces_of(s, refs[:4])):
        stage[i] = ref[start : start + FF_BLOCK, :].astype(f32)
        column = pl.multiple_of((2 * group + core) * FF_BLOCK, FF_BLOCK)
        row = pl.multiple_of(half * HALF, HALF)
        copies += [
            pltpu.make_async_copy(stage.at[i, 0:HALF], down_any.at[pl.ds(column + row, HALF)], sems.at[2 * i]),
            pltpu.make_async_copy(
                stage.at[i, HALF:], up_any.at[pl.ds(row, HALF), pl.ds(column, FF_BLOCK)], sems.at[2 * i + 1]
            ),
        ]
        copies[-1].start()
        copies[-2].start()
    for copy in copies:
        copy.wait()


def final_conv_kernel(base, chosen, small, s, *refs):
    if small:
        conv_any, *vec_refs, freq_ref, mark, stage, sems, lines, table = refs[-(small + 7) :]
    else:
        conv_any, mark, stage, sems = refs[-4:]
    mark[...] = jnp.zeros_like(mark)
    copies = []
    rows = stage.shape[1]
    width = stage.shape[2]
    quarters = refs[:4]
    for i, (ref, half, core) in enumerate(pieces_of(s, quarters)):
        if i not in chosen:
            continue
        stage[i] = ref[0:rows, :].astype(f32)
        row = pl.multiple_of(base + half * rows, HALF)
        copies.append(
            pltpu.make_async_copy(
                stage.at[i], conv_any.at[pl.ds(row, rows), pl.ds(pl.multiple_of(core * width, width), width)], sems.at[i]
            )
        )
        copies[-1].start()
    if small:
        own, recv, other_own, other_recv = (r[rows:, :].astype(f32) for r in quarters)
        total = (own + recv) + (other_own + other_recv)
        row = 0
        for i, ref in enumerate(vec_refs):
            for j in range(ref.shape[1] // width):
                lines[i : i + 1, j * width : (j + 1) * width] = total[row : row + 1, :]
                row += 1
            copies.append(pltpu.make_async_copy(lines.at[i : i + 1, 0 : ref.shape[1]], ref, sems.at[4 + i]))
            copies[-1].start()
        table[...] = total[row : row + SPECIES, 0 : freq_ref.shape[1]] / WINDOW_BASES
        copies.append(pltpu.make_async_copy(table, freq_ref, sems.at[4 + small]))
        copies[-1].start()
    for copy in copies:
        copy.wait()


class Group:
    def __init__(self, name, calls, scheme):
        self.name, self.calls, self.scheme, self.small = name, calls, scheme, None
        self.stage = 0
        self.pairs, self.recvs = [], []

    def send_first(self, send):
        self.recvs.append(exchange(send, self.scheme[0][1]))
        self.calls.follows(send)

    def keep_first(self, keep):
        self.pairs.append((keep, self.recvs.pop(0)))

    def step(self):
        stage, calls = self.stage, self.calls
        name = f"sum_{self.name}{stage}"
        kind, bits = self.scheme[stage]
        if stage + 1 == len(self.scheme):
            self.others.append(swap_cores(self.recv))
            calls.also += [self.recv, self.others[0]]
            self.quarters = [(v, "v") for v in (self.send, self.recv, *self.others)]
            return
        next_kind, next_bits = self.scheme[stage + 1]
        pairs = self.pairs if stage == 0 else [(self.keep, self.recv)]
        ins = [(v, "v") for pair in pairs for v in pair]
        rows, width = sum(p[0].shape[0] for p in pairs), pairs[0][1].shape[1]
        if next_kind == "halve":
            half = ((rows // 2, width), bf16, "v")
            self.keep, self.send = calls(
                functools.partial(split_kernel, PLACE_OF[next_bits]), name, [half, half], ins,
                scratch=[pltpu.VMEM((rows, width), bf16)] if len(pairs) > 1 else [],
            )
        else:
            small = self.small if kind == "halve" and self.small is not None else None
            behind = SMALL_ROWS if self.small is not None else 0
            if kind == "join":
                h = rows - behind
                kernel, rows = functools.partial(join_kernel, h, PLACE_OF[bits]), 2 * h + behind
            else:
                kernel = sum_kernel
                if small is not None:
                    ins.append((small, "v"))
                    rows += behind
            (self.send,) = calls(kernel, name, [((rows, width), bf16, "v")], ins)
            count = lax.axis_size("batch")
            if kind != "join" and next_kind == "join" and count > 16:
                others = [[j + 16 * i for i in range(count // 16)] for j in range(16)]
                self.send = lax.psum(self.send, "batch", axis_index_groups=others)
            self.keep = self.send
        self.stage += 1
        self.recv = exchange(self.send, next_bits)
        calls.follows(self.send)
        if self.stage + 1 == len(self.scheme):
            self.others = [swap_cores(self.send)]


CONV_BLOCKS = (5, 4)
GROUPS = {"a": "a", "b": "b", "c": "c", "d": "d"}
SCHEMES = {"a": SHORT, "b": SHORT, "c": LONG, "d": LONG}
PLAN = (
    "R0", "R1", "F", "a", "b", "Dcs", "a", "Dck", "Dds", "b", "Ddk", "c", "a", "E0", "d", "c", "b", "a", "d",
    "c", "E1", "S", "b", "d", "a", "c", "b", "d", "a", "c", "b", "d", "c", "fb", "d", "fa", "gd", "gc", "c",
    "d", "fc", "fd",
)


def body(
    inputs,
    conv_weight,
    conv_bias,
    norm1_gain,
    norm1_shift,
    norm2_gain,
    norm2_shift,
    up_weight,
    up_bias,
    down_weight,
    down_bias,
    head_weight,
    species,
    cotangent,
):
    nw, seg, d = inputs.shape
    taps = conv_weight.shape[0]
    ff = up_weight.shape[1]
    rows = nw * seg
    rim = (taps - 1) // 2 * DILATION_STEP
    calls = Calls()
    head = head_weight.T
    ub = up_bias.reshape(1, ff)
    xp = swap_cores(inputs)
    win = (nw, seg, d)
    sides = ((2, nw, seg + 2 * rim, d), bf16, "v")
    six = [v.reshape(1, d) for v in (conv_bias, norm1_gain, norm1_shift, norm2_gain, norm2_shift, down_bias)]
    a, both, w, x, vectors = calls(
        functools.partial(prepare_kernel, rim),
        "prepare",
        [((nw, 2 * seg, d), bf16, "v"), sides, (conv_weight.shape, bf16, "v"), (win, bf16, "v"), ((8, d), f32, "v")],
        [(v, "a") for v in (inputs, conv_weight, *six)],
        scratch=[pltpu.VMEM((nw, seg + 2 * rim, d), f32), pltpu.SemaphoreType.DMA((6 + nw + taps,))],
    )
    h, gp, n, dy, up, down, _ = calls(
        functools.partial(conv_kernel, rim),
        "conv_forward",
        [
            (win, f32, "v"), (win, f32, "v"), (win, bf16, "v"), (win, bf16, "v"),
            (up_weight.shape, bf16, "v"), (down_weight.shape, bf16, "v"), sides,
        ],
        [(v, "v") for v in (xp, both, w, x, vectors)] + [(v, "a") for v in (cotangent, up_weight, down_weight)],
        scratch=[pltpu.SemaphoreType.DMA((3,))],
        aliases={1: 6},
    )
    h, gp, n, dyr = (v.reshape(rows, d) for v in (h, gp, n, dy))

    wide = ((rows, FF_BLOCK), bf16, "v")
    recvs = []
    groups = {name: Group(name, calls, SCHEMES[name]) for name in GROUPS}
    owner = {member: groups[name] for name, members in GROUPS.items() for member in members}
    starts = {members[i]: i * FF_BLOCK for members in GROUPS.values() for i in range(len(members))}
    qs, dzs = [], []
    ubg = None
    for index in range(4):
        ins = [n, dyr, up, ub, down]
        if index >= 2:
            ins.append(recvs[index - 2])
        if index:
            ins.append(ubg)
        outs = [((FF_BLOCK, d), bf16, "v")] * 2 if index >= 2 else [((2 * FF_BLOCK, d), bf16, "v")]
        *res, q, dz, ubg = calls(
            functools.partial(ffn_kernel, index),
            f"ffn_{index}",
            outs + [wide, wide, ((1, ff), f32, "v")],
            [(v, "v") for v in ins],
            scratch=[pltpu.VMEM((2 * FF_BLOCK, d), f32)],
            limit=8,
        )
        qs.append(q)
        dzs.append(dz)
        if index >= 2:
            owner["ab"[index - 2]].send_first(res[1])
            owner["ab"[index - 2]].keep_first(res[0])
        else:
            recvs.append(swap_cores(res[0]))
            calls.follows(res[0])
    after = []

    bases = {"c": 0, "d": 2 * CONV_BLOCKS[0]}
    assert 2 * sum(CONV_BLOCKS) == 2 * taps
    half = d // 2
    extent = 2 * seg + 2 * rim
    both = None
    input_grad = sums1 = None
    final = {}
    for item in PLAN:
        if item[0] == "R":
            ins = [dyr, up, down, h, gp, vectors, *qs, *dzs]
            outs = [((rows, d), bf16, "v"), ((rows, d), f32, "v"), ((rows, d), bf16, "v"), ((4, d), f32, "v")]
            if item == "R0":
                aliases = {len(ins) + 1: 4}
                ins += [xp, a]
                outs.append((a.shape, bf16, "v"))
            else:
                aliases = {len(ins) + i: i for i in range(4)}
                ins += after
            *after, last = calls(
                functools.partial(rows_kernel, int(item[1])), f"rows_{item[1]}", outs, [(v, "v") for v in ins], aliases=aliases
            )
            if item == "R0":
                a = last
            else:
                act, dh, du = after
                sums2 = last
                du, dh = du.reshape(win), dh.reshape(win)
                dup = swap_cores(du)
                calls.follows(du)
        elif item == "F":
            act_out, freq = calls(
                head_kernel,
                "head",
                [((rows, d), bf16, "a"), ((SPECIES, 128), f32, "v")],
                [(act, "v"), (head, "v"), (species.reshape(1, nw), "v")],
                scratch=[pltpu.SemaphoreType.DMA((1,)), pltpu.VMEM((128, d), bf16)],
            )
        elif item[0] == "D":
            g = item[1]
            blocks = CONV_BLOCKS["cd".index(g)]
            kernel = functools.partial(conv_weight_kernel, rim, bases[g], blocks, item[2] == "k", both is None)
            outs = [((blocks * half, half), bf16, "v")]
            ins = [(a, "v"), (du, "v"), (dup, "v")]
            if both is None:
                outs.append(((2, nw, extent, half), bf16, "v"))
                part, both = calls(kernel, f"conv_weight_{item}", outs, ins, scratch=[pltpu.VMEM((extent, half), f32)] * nw)
            else:
                (part,) = calls(kernel, f"conv_weight_{item}", outs, ins + [(both, "v")])
            if item[2] == "s":
                owner[g].send_first(part)
            else:
                owner[g].keep_first(part)
        elif item[0] == "E":
            windows = (0, 1) if item == "E0" else (2, 3)
            ins = [(du, "v"), (dup, "v"), (conv_weight, "a") if item == "E0" else (w, "v"), (dh, "v"), (x, "v"), (vectors, "v")]
            outs = [(win, bf16, "a"), ((2, d), f32, "v")]
            aliases = None
            if item == "E0":
                outs.append((conv_weight.shape, bf16, "v"))
            else:
                aliases = {len(ins): 0}
                ins += [(input_grad, "a"), (sums1, "v")]
            input_grad, sums1, *more = calls(
                functools.partial(conv_input_kernel, rim, windows),
                f"conv_input_{windows[0]}",
                outs,
                ins,
                scratch=[pltpu.VMEM((2, seg, d), bf16), pltpu.SemaphoreType.DMA((2 + taps,))]
                + window_scratch(2, seg, rim, d),
                limit=12,
                aliases=aliases,
            )
            if more:
                (w,) = more
        elif item == "S":
            (owner["d"].small,) = calls(
                small_kernel, "small", [((SMALL_ROWS, half), f32, "v")], [(sums2, "v"), (sums1, "v"), (ubg, "v"), (freq, "v")]
            )
        elif item[0] in "fg":
            g = owner[item[1]]
            if item[1] in "ab":
                prev = final.get("ffn", ())[:2]
                final["ffn"] = calls(
                    functools.partial(final_ffn_kernel, "ab".index(item[1]), starts[item[1]]),
                    f"final_{item[1]}",
                    [(down_weight.shape, f32, "a"), (up_weight.shape, f32, "a"), MARK],
                    g.quarters + [(p, "a") for p in prev],
                    scratch=[pltpu.VMEM((4, FF_BLOCK, d), f32), pltpu.SemaphoreType.DMA((8,))],
                    limit=10,
                    aliases={4 + i: i for i in range(len(prev))},
                )
            else:
                prev = final.get("conv", ())[:1]
                early, last = item[0] == "g", item[1] == "d" and item[0] == "f"
                chosen = (0, 2) if early else (1, 3) if "g" + item[1] in PLAN else (0, 1, 2, 3)
                small = [d] * 6 + [ff] if last else []
                outs = [((taps * d, d), f32, "a")] + [((1, k), f32, "a") for k in small]
                outs += [((SPECIES, head_weight.shape[1]), f32, "a")] if small else []
                outs.append(MARK)
                more = [pltpu.VMEM((len(small), ff), f32), pltpu.VMEM((SPECIES, head_weight.shape[1]), f32)] if small else []
                quarters = [(g.send, "v"), (g.send, "v"), (g.others[0], "v"), (g.others[0], "v")] if early else g.quarters
                final["conv"] = calls(
                    functools.partial(final_conv_kernel, bases[item[1]] * half, chosen, len(small)),
                    f"final_{item}",
                    outs,
                    quarters + [(p, "a") for p in prev],
                    scratch=[
                        pltpu.VMEM((4, CONV_BLOCKS["cd".index(item[1])] * half, half), f32),
                        pltpu.SemaphoreType.DMA((5 + len(small),)),
                    ]
                    + more,
                    limit=10,
                    aliases={4: 0} if prev else None,
                )
        else:
            groups[item].step()
    down_grad, up_grad, _ = final["ffn"]
    conv_grad, conv_b, g2, s2, down_b, g1, s1, up_b, frequencies, _ = final["conv"]
    return (
        act_out.reshape(win),
        input_grad,
        conv_grad.reshape(taps, d, d),
        conv_b.reshape(d),
        g1.reshape(d),
        s1.reshape(d),
        g2.reshape(d),
        s2.reshape(d),
        up_grad,
        up_b.reshape(ff),
        down_grad,
        down_b.reshape(d),
        frequencies,
    )


def solution(mesh):
    rows = P("batch", "seq", None)
    placed = (rows,) + (P(),) * 11 + (P("batch"), rows)
    return jax.shard_map(
        body, mesh=mesh, in_specs=placed, out_specs=(rows, rows) + (P(),) * 11, check_vma=False
    )
```

```python
import functools

import jax
import jax.numpy as jnp
from jax import lax
from jax.experimental import pallas as pl
from jax.experimental.pallas import tpu as pltpu
from jax.sharding import PartitionSpec as P

DILATION_STEP = 8
WINDOW_BASES = 512
SPECIES = 8
EPS = 1e-05
MB = 1 << 20
f32 = jnp.float32
bf16 = jnp.bfloat16

IN_VMEM = pl.BlockSpec(memory_space=pltpu.VMEM)
ANYWHERE = pl.BlockSpec(memory_space=pl.ANY)

BIT0, BIT1, BIT2, CORE, OTHER_BIT0 = range(5)

PLANE, ACROSS, NEAR, FAR = (0, 1), (1, 0), (2, 2), (3, 3)
LONG = (
    ("halve", PLANE), ("halve", ACROSS), ("halve", NEAR), ("whole", FAR),
    ("join", NEAR), ("join", ACROSS), ("join", PLANE),
)
SHORT = (
    ("halve", PLANE), ("halve", ACROSS), ("whole", (2, 3)), ("whole", (3, 2)),
    ("join", ACROSS), ("join", PLANE),
)
PLACE_OF = {PLANE: BIT0, ACROSS: BIT1, NEAR: BIT2}


def normal_parts(u):
    return 0.5 + 0.5 * lax.erf(u * 0.5**0.5), u * (jnp.exp(-0.5 * (u * u)) * 0.3989422804014327)


def centred(value):
    centre = value - jnp.mean(value, axis=-1, keepdims=True)
    scale = lax.rsqrt(jnp.mean(centre * centre, axis=-1, keepdims=True) + EPS)
    return centre * scale, scale


def norm_back(grad, hat, scale):
    return scale * (grad - jnp.mean(grad, axis=-1, keepdims=True) - hat * jnp.mean(grad * hat, axis=-1, keepdims=True))


def contract(a, b, dim_a, dim_b):
    return lax.dot_general(a, b, (((dim_a,), (dim_b,)), ((), ())), preferred_element_type=f32)


def column_sum(value):
    return jnp.sum(value, axis=0, keepdims=True)


def added(total, value):
    return value if total is None else total + value


MARK = ((8, 128), f32, "v")


def places_here():
    core = lax.axis_index("seq")
    place = lax.axis_index("batch")

    def bit(bits, at):
        return lax.shift_right_logical(place, bits[0] + at * (bits[1] - bits[0])) & 1

    return bit(PLANE, core), bit(ACROSS, core), bit(NEAR, core), core, bit(PLANE, 1 - core)


class Calls:
    def __init__(self):
        self.last = None
        self.also = []

    def __call__(self, kernel, name, outs, ins, scratch=(), limit=8, aliases=None):
        count = len(ins)
        tokens = self.also + ([] if self.last is None else [self.last])
        self.also = []

        def run(*refs):
            kernel(places_here(), *refs[:count], *refs[count + len(tokens) :])

        places = {"v": pltpu.VMEM, "a": pltpu.HBM}
        values = [pltpu.with_memory_space_constraint(x, places[w]) if w in places else x for x, w in ins]
        result = pl.pallas_call(
            run,
            out_shape=tuple(places[w](s, d) for s, d, w in outs),
            in_specs=[{"v": IN_VMEM, "a": ANYWHERE}[w] for _, w in ins] + [ANYWHERE] * len(tokens),
            out_specs=tuple(IN_VMEM if w == "v" else ANYWHERE for _, _, w in outs),
            scratch_shapes=list(scratch),
            input_output_aliases=aliases or {},
            compiler_params=pltpu.CompilerParams(vmem_limit_bytes=limit * MB),
            cost_estimate=pl.CostEstimate(flops=20*10**9, bytes_accessed=1, transcendentals=0),
            name=name,
        )(*values, *tokens)
        result = tuple(result)
        self.last = min(result, key=lambda x: x.size)
        return result

    def follows(self, value):
        self.also.append(value)


def window_scratch(count, seg, rim, width):
    extent = seg + 2 * rim
    return [pltpu.VMEM((extent, width), f32) for _ in range(count)] + [
        pltpu.VMEM((2, extent, width), bf16) for _ in range(count)
    ]


def fill_segment(pad, both, core, rim, own, other):
    seg = own.shape[0]
    extent = seg + 2 * rim
    pad[0:rim, :] = jnp.where(core == 0, 0.0, other[seg - rim :, :])
    pad[rim : rim + seg, :] = own
    pad[rim + seg :, :] = jnp.where(core == 0, other[0:rim, :], 0.0)
    both[0] = pad[...].astype(bf16)
    both[1, 0 : extent - 16, :] = pad[8 : extent - 8, :].astype(bf16)


def prepare_kernel(rim, s, x_any, w_any, *refs):
    vec_anys, (a_ref, both_ref, w_ref, x_ref, vec_ref, pad, sems) = refs[:6], refs[6:]
    nw, seg, d = x_ref.shape
    extent = seg + 2 * rim
    core = s[CORE]
    copies = [pltpu.make_async_copy(v, vec_ref.at[i : i + 1], sems.at[i]) for i, v in enumerate(vec_anys)]
    copies += [pltpu.make_async_copy(x_any.at[i], x_ref.at[i], sems.at[6 + i]) for i in range(nw)]
    weights = [pltpu.make_async_copy(w_any.at[k], w_ref.at[k], sems.at[6 + nw + k]) for k in range(w_ref.shape[0])]
    for copy in copies + weights:
        copy.start()
    for copy in copies[:6]:
        copy.wait()
    for w in range(nw):
        copies[6 + w].wait()
        own = centred(x_ref[w].astype(f32))[0] * vec_ref[1:2, :] + vec_ref[2:3, :]
        pad[w, rim : rim + seg, :] = own
        own = own.astype(bf16)
        a_ref[w, pl.ds(pl.multiple_of(core * seg, seg), seg), :] = own
        both_ref[0, w, rim : rim + seg, :] = own
        both_ref[1, w, rim : rim + seg - 16, :] = pad[w, rim + 8 : rim + seg - 8, :].astype(bf16)
    for copy in weights:
        copy.wait()


def set_rims(both_ref, w, core, rim, seg, near_left, near_right):
    left = jnp.where(core == 0, 0.0, near_left)
    right = jnp.where(core == 0, near_right, 0.0)
    end = rim + seg
    both_ref[0, w, 0:rim, :] = left.astype(bf16)
    both_ref[0, w, end : end + rim, :] = right.astype(bf16)
    first = both_ref[0, w, rim : rim + 16, :].astype(f32)[0:8]
    last = both_ref[0, w, end - 16 : end, :].astype(f32)[8:16]
    both_ref[1, w, 0:rim, :] = jnp.concatenate([left[8:], first], axis=0).astype(bf16)
    both_ref[1, w, end - 16 : end + rim - 16, :] = jnp.concatenate([last, right[: rim - 8]], axis=0).astype(bf16)


def conv_kernel(rim, s, xp_ref, both_in, w_ref, x_ref, vec_ref, dy_any, up_any, down_any, h_ref, gp_ref, n_ref, dy_ref, up_ref, down_ref, both_ref, sems):
    nw, seg, _ = x_ref.shape
    taps = w_ref.shape[0]
    core = s[CORE]
    copies = [
        pltpu.make_async_copy(a, b, sems.at[i])
        for i, (a, b) in enumerate(((dy_any, dy_ref), (up_any, up_ref), (down_any, down_ref)))
    ]
    for copy in copies:
        copy.start()
    bias, g1, s1, g2, s2 = (vec_ref[i : i + 1, :] for i in range(5))

    def rims(w):
        near_left = centred(xp_ref[w, seg - rim :, :].astype(f32))[0] * g1 + s1
        near_right = centred(xp_ref[w, 0:rim, :].astype(f32))[0] * g1 + s1
        set_rims(both_ref, w, core, rim, seg, near_left, near_right)

    def finish(w, u):
        x = x_ref[w].astype(f32)
        cdf, slope = normal_parts(u)
        h = x + u * cdf
        gp_ref[w] = cdf + slope
        h_ref[w] = h
        n_ref[w] = (centred(h)[0] * g2 + s2).astype(bf16)

    for w in range(nw):
        rims(w)
    before = None
    for w in range(nw):
        u = bias
        for k in range(taps):
            start = (k - k % 2) * DILATION_STEP
            u = u + jnp.dot(both_ref[k % 2, w, start : start + seg, :], w_ref[k], preferred_element_type=f32)
            if k == 4 and before is not None:
                finish(w - 1, before)
        before = u
    finish(nw - 1, before)
    for copy in copies:
        copy.wait()


FF_BLOCK = 512
CHUNK = 256
COLS = 256
HALF = FF_BLOCK // 2


def block_column(number, core):
    return pl.multiple_of(((number % 2) * 2 + (core if number >= 2 else 1 - core)) * FF_BLOCK, FF_BLOCK)


def ffn_kernel(index, s, n_ref, dy_ref, up_ref, ub_ref, down_ref, *refs):
    keeps = index >= 2
    if keeps:
        recv_ref, ubg_in, keep_ref, send_ref, q_s, dz_s, ubg_ref, part_s = refs
    elif index:
        ubg_in, send_ref, q_s, dz_s, ubg_ref, part_s = refs
    else:
        send_ref, q_s, dz_s, ubg_ref, part_s = refs
    rows = n_ref.shape[0]
    chunks = rows // CHUNK
    parts = FF_BLOCK // COLS
    column = block_column(index, s[CORE])
    total = [None] * parts

    def early(chunk, part):
        r = slice(chunk * CHUNK, (chunk + 1) * CHUNK)
        c = pl.ds(pl.multiple_of(column + part * COLS, COLS), COLS)
        z = jnp.dot(n_ref[r, :], up_ref[:, c], preferred_element_type=f32) + ub_ref[:, c]
        dq = contract(dy_ref[r, :], down_ref[c, :], 1, 1)
        cdf, slope = normal_parts(z)
        here = slice(part * COLS, (part + 1) * COLS)
        q_s[r, here] = (z * cdf).astype(bf16)
        dz = dq * (cdf + slope)
        dz_s[r, here] = dz.astype(bf16)
        total[part] = added(total[part], column_sum(dz))

    def weights(stage, piece):
        kept, of_up = piece // 2, piece % 2
        half = (s[BIT0] if kept else 1 - s[BIT0]) if keeps else kept
        lanes = pl.ds(pl.multiple_of(half * HALF, HALF), HALF)
        r = slice(stage * rows // 2, (stage + 1) * rows // 2)
        if of_up:
            g = contract(n_ref[r, lanes], dz_s[r, :], 0, 0)
        else:
            g = contract(q_s[r, lanes], dy_ref[r, :], 0, 0)
        place = slice(piece * HALF, (piece + 1) * HALF)
        if stage == 0:
            part_s[place, :] = g
            return
        g = g + part_s[place, :]
        if not keeps:
            send_ref[place, :] = g.astype(bf16)
            return
        g = g + recv_ref[pl.ds(pl.multiple_of((half * 2 + of_up) * HALF, HALF), HALF), :].astype(f32)
        (keep_ref if kept else send_ref)[of_up * HALF : (of_up + 1) * HALF, :] = g.astype(bf16)

    queue = []
    for chunk in range(chunks):
        for part in range(parts):
            early(chunk, part)
            if queue:
                queue.pop(0)()
        if chunk == chunks // 2 - 1:
            queue += [functools.partial(weights, 0, p) for p in range(4)]
    for p in range(4):
        weights(1, p)
    ubg_ref[...] = ubg_in[...] if index else jnp.zeros_like(ubg_ref)
    for part in range(parts):
        ubg_ref[:, pl.ds(pl.multiple_of(column + part * COLS, COLS), COLS)] = total[part]


def rows_kernel(half, s, dy_ref, up_ref, down_ref, h_ref, gp_ref, vec_ref, *refs):
    q_refs, dz_refs, refs = refs[:4], refs[4:8], refs[8:]
    if half:
        act_in, dh_in, du_in, sums_in, *refs = refs
    else:
        xp_ref, a_in, *refs, a_ref = refs
    act_ref, dh_ref, du_ref, sums_ref = refs
    core = s[CORE]
    rows = dy_ref.shape[0]
    sums = [None] * 4

    def norm_other(w):
        seg = xp_ref.shape[1]
        other = centred(xp_ref[w].astype(f32))[0] * vec_ref[1:2, :] + vec_ref[2:3, :]
        a_ref[w, pl.ds(pl.multiple_of((1 - core) * seg, seg), seg), :] = other.astype(bf16)

    def products(r):
        out = dn = None
        for number in range(4):
            c = pl.ds(block_column(number, core), FF_BLOCK)
            out = added(out, jnp.dot(q_refs[number][r, :], down_ref[c, :], preferred_element_type=f32))
            dn = added(dn, contract(dz_refs[number][r, :], up_ref[:, c], 1, 1))
        return out, dn

    def finish(r, out, dn):
        h = h_ref[r, :]
        dy = dy_ref[r, :].astype(f32)
        act_ref[r, :] = (h + out + vec_ref[5:6, :]).astype(bf16)
        hat, scale = centred(h)
        dh = dy + norm_back(dn * vec_ref[3:4, :], hat, scale)
        dh_ref[r, :] = dh
        du = dh * gp_ref[r, :]
        du_ref[r, :] = du.astype(bf16)
        for i, v in enumerate((du, dn * hat, dn, dy)):
            sums[i] = added(sums[i], column_sum(v))

    before = None
    for chunk in range(half * rows // CHUNK // 2, (half + 1) * rows // CHUNK // 2):
        r = slice(chunk * CHUNK, (chunk + 1) * CHUNK)
        now = products(r)
        if not half:
            for w in range(chunk * 2, chunk * 2 + 2):
                norm_other(w)
        if before is not None:
            finish(*before)
        before = (r, *now)
    finish(*before)
    for i in range(4):
        sums_ref[i : i + 1, :] = sums_in[i : i + 1, :] + sums[i] if half else sums[i]


def conv_weight_kernel(rim, first_block, blocks, kept, fills, s, a_ref, du_ref, dup_ref, *refs):
    if fills:
        out_ref, both, *pads = refs
    else:
        both, out_ref = refs
    core = s[CORE]
    nw, seg, d = du_ref.shape
    half = d // 2
    extent = 2 * seg + 2 * rim
    cols = pl.ds(pl.multiple_of(core * half, half), half)
    if fills:
        for w in range(nw):
            pad = pads[w]
            zeros = jnp.zeros((rim, half), f32)
            pad[0:rim, :] = zeros
            pad[extent - rim : extent, :] = zeros
            pad[pl.ds(pl.multiple_of(rim + core * seg, 16), seg), :] = du_ref[w, :, cols].astype(f32)
            pad[pl.ds(pl.multiple_of(rim + (1 - core) * seg, 16), seg), :] = dup_ref[w, :, cols].astype(f32)
            both[0, w] = pad[...].astype(bf16)
            both[1, w, 0 : extent - 16, :] = pad[8 : extent - 8, :].astype(bf16)
    part = s[BIT0] if kept else 1 - s[BIT0]
    for i in range(blocks):
        block = first_block + part * blocks + i
        tap = block // 2
        odd = lax.rem(tap, 2)
        lanes = pl.ds(pl.multiple_of(lax.rem(block, 2) * half, half), half)
        start = pl.multiple_of(2 * rim - (tap + odd) * DILATION_STEP, 16)
        right = both[odd, :, pl.ds(start, 2 * seg), :].reshape(nw * 2 * seg, half)
        left = a_ref[:, :, lanes].reshape(nw * 2 * seg, half)
        out_ref[i * half : (i + 1) * half, :] = contract(left, right, 0, 0).astype(bf16)


def conv_input_kernel(rim, windows, s, du_ref, dup_ref, w_ref, dh_ref, x_ref, vec_ref, *refs):
    if windows[0]:
        grad_in, sums_in, grad_any, sums_ref, grad, sem, *scratch = refs
    else:
        grad_any, sums_ref, w_out, grad, sem, *scratch = refs
        loads = [pltpu.make_async_copy(w_ref.at[k], w_out.at[k], sem.at[2 + k]) for k in range(w_out.shape[0])]
        for load in loads:
            load.start()
        w_ref = w_out
    seg = x_ref.shape[1]
    core = s[CORE]
    count = len(windows)
    pads, boths = scratch[:count], scratch[count:]
    totals = [None, None]
    copies = []

    def prepare(i):
        fill_segment(pads[i], boths[i], core, rim, du_ref[windows[i]].astype(f32), dup_ref[windows[i]].astype(f32))

    def finish(i, da):
        w = windows[i]
        hat, scale = centred(x_ref[w].astype(f32))
        grad[i] = (dh_ref[w] + norm_back(da * vec_ref[1:2, :], hat, scale)).astype(bf16)
        copies.append(pltpu.make_async_copy(grad.at[i], grad_any.at[w], sem.at[i]))
        copies[-1].start()
        totals[0] = added(totals[0], column_sum(da * hat))
        totals[1] = added(totals[1], column_sum(da))

    prepare(0)
    before = None
    for i in range(count):
        da = None
        for k in range(w_ref.shape[0]):
            if i == 0 and not windows[0]:
                loads[k].wait()
            start = 2 * rim - (k + k % 2) * DILATION_STEP
            da = added(da, contract(boths[i][k % 2, start : start + seg, :], w_ref[k], 1, 1))
            if k == 2 and i + 1 < count:
                prepare(i + 1)
            if k == 5 and before is not None:
                finish(i - 1, before)
        before = da
    finish(count - 1, before)
    for i in range(2):
        sums_ref[i : i + 1, :] = totals[i] + sums_in[i : i + 1, :] if windows[0] else totals[i]
    for copy in copies:
        copy.wait()


SMALL_ROWS = 32


def head_kernel(s, act_ref, head_ref, species_ref, act_any, freq_ref, sem, head_s):
    copy = pltpu.make_async_copy(act_ref, act_any, sem.at[0])
    copy.start()
    classes = head_ref.shape[0]
    head_s[...] = jnp.zeros_like(head_s)
    head_s[0:classes, :] = head_ref[...]
    nw = species_ref.shape[1]
    logits = contract(act_ref[...], head_s[...], 1, 1)
    lane = lax.broadcasted_iota(jnp.int32, logits.shape, 1)
    logits = jnp.where(lane < classes, logits, -jnp.inf)
    e = jnp.exp(logits - jnp.max(logits, axis=-1, keepdims=True))
    probs = e / jnp.sum(e, axis=-1, keepdims=True)
    seg = logits.shape[0] // nw
    row = lax.broadcasted_iota(jnp.int32, freq_ref.shape, 0)
    freq = jnp.zeros(freq_ref.shape, f32)
    for w in range(nw):
        freq = freq + jnp.where(row == species_ref[0:1, w : w + 1], column_sum(probs[w * seg : (w + 1) * seg, :]), 0.0)
    freq_ref[...] = freq
    copy.wait()


def small_kernel(s, sums2_ref, sums1_ref, ubg_ref, freq_ref, out_ref):
    out_ref[...] = jnp.zeros_like(out_ref)
    vectors = [sums2_ref[i : i + 1, :] for i in range(4)] + [sums1_ref[i : i + 1, :] for i in range(2)]
    vectors += [ubg_ref[:, i * 512 : (i + 1) * 512] for i in range(ubg_ref.shape[1] // 512)]
    width = out_ref.shape[1]
    for i, v in enumerate(vectors):
        for j in range(2):
            out_ref[2 * i + j : 2 * i + j + 1, :] = v[:, j * width : (j + 1) * width]
    out_ref[2 * len(vectors) : 2 * len(vectors) + SPECIES, 0 : freq_ref.shape[1]] = freq_ref[...]


def swap_cores(value):
    return lax.ppermute(value, "seq", [(0, 1), (1, 0)])


def exchange(value, bits):
    count = lax.axis_size("batch")
    pairs = [(c * count + i, c * count + (i ^ (1 << bits[c]))) for c in range(2) for i in range(count)]
    return lax.ppermute(value, ("seq", "batch"), pairs)


def add16(a, b):
    return (a.astype(f32) + b.astype(f32)).astype(bf16)


def split_kernel(bit, s, *refs):
    if len(refs) == 4:
        keep_ref, recv_ref, keep_out, send_out = refs
        h = keep_out.shape[0]
        for out, half in ((send_out, 1 - s[bit]), (keep_out, s[bit])):
            r = pl.ds(pl.multiple_of(half * h, 16), h)
            out[...] = add16(keep_ref[r, :], recv_ref[r, :])
        return
    *pairs, keep_out, send_out, whole = refs
    at = 0
    for keep_ref, recv_ref in zip(pairs[::2], pairs[1::2]):
        rows = keep_ref.shape[0]
        whole[at : at + rows, :] = add16(keep_ref[...], recv_ref[...])
        at += rows
    h = keep_out.shape[0]
    for out, half in ((send_out, 1 - s[bit]), (keep_out, s[bit])):
        out[...] = whole[pl.ds(pl.multiple_of(half * h, 16), h), :]


def sum_kernel(s, keep_ref, recv_ref, *refs):
    out_ref = refs[-1]
    h = keep_ref.shape[0]
    out_ref[0:h, :] = add16(keep_ref[...], recv_ref[...])
    if len(refs) == 2:
        out_ref[h:, :] = refs[0][...].astype(bf16)


def join_kernel(h, bit, s, own_ref, recv_ref, out_ref):
    for ref, half in ((own_ref, s[bit]), (recv_ref, 1 - s[bit])):
        out_ref[pl.ds(pl.multiple_of(half * h, 16), h), :] = ref[0:h, :]
    if out_ref.shape[0] > 2 * h:
        out_ref[2 * h :, :] = add16(own_ref[h:, :], recv_ref[h:, :])


def copy_kernel(s, in_ref, out_ref):
    out_ref[...] = in_ref[...]


def pieces_of(s, refs):
    core = s[CORE]
    places = (s[BIT0], core), (1 - s[BIT0], core), (s[OTHER_BIT0], 1 - core), (1 - s[OTHER_BIT0], 1 - core)
    return [(r, h, c) for r, (h, c) in zip(refs, places)]


def final_ffn_kernel(group, start, s, *refs):
    down_any, up_any, mark, stage, sems = refs[-5:]
    mark[...] = jnp.zeros_like(mark)
    copies = []
    for i, (ref, half, core) in enumerate(pieces_of(s, refs[:4])):
        stage[i] = ref[start : start + FF_BLOCK, :].astype(f32)
        column = pl.multiple_of((2 * group + core) * FF_BLOCK, FF_BLOCK)
        row = pl.multiple_of(half * HALF, HALF)
        copies += [
            pltpu.make_async_copy(stage.at[i, 0:HALF], down_any.at[pl.ds(column + row, HALF)], sems.at[2 * i]),
            pltpu.make_async_copy(
                stage.at[i, HALF:], up_any.at[pl.ds(row, HALF), pl.ds(column, FF_BLOCK)], sems.at[2 * i + 1]
            ),
        ]
        copies[-1].start()
        copies[-2].start()
    for copy in copies:
        copy.wait()


def final_conv_kernel(base, chosen, small, s, *refs):
    if small:
        conv_any, *vec_refs, freq_ref, mark, stage, sems, lines, table = refs[-(small + 7) :]
    else:
        conv_any, mark, stage, sems = refs[-4:]
    mark[...] = jnp.zeros_like(mark)
    copies = []
    rows = stage.shape[1]
    width = stage.shape[2]
    quarters = refs[:4]
    for i, (ref, half, core) in enumerate(pieces_of(s, quarters)):
        if i not in chosen:
            continue
        stage[i] = ref[0:rows, :].astype(f32)
        row = pl.multiple_of(base + half * rows, HALF)
        copies.append(
            pltpu.make_async_copy(
                stage.at[i], conv_any.at[pl.ds(row, rows), pl.ds(pl.multiple_of(core * width, width), width)], sems.at[i]
            )
        )
        copies[-1].start()
    if small:
        own, recv, other_own, other_recv = (r[rows:, :].astype(f32) for r in quarters)
        total = (own + recv) + (other_own + other_recv)
        row = 0
        for i, ref in enumerate(vec_refs):
            for j in range(ref.shape[1] // width):
                lines[i : i + 1, j * width : (j + 1) * width] = total[row : row + 1, :]
                row += 1
            copies.append(pltpu.make_async_copy(lines.at[i : i + 1, 0 : ref.shape[1]], ref, sems.at[4 + i]))
            copies[-1].start()
        table[...] = total[row : row + SPECIES, 0 : freq_ref.shape[1]] / WINDOW_BASES
        copies.append(pltpu.make_async_copy(table, freq_ref, sems.at[4 + small]))
        copies[-1].start()
    for copy in copies:
        copy.wait()


class Group:
    def __init__(self, name, calls, scheme):
        self.name, self.calls, self.scheme, self.small = name, calls, scheme, None
        self.stage = 0
        self.pairs, self.recvs = [], []

    def send_first(self, send):
        self.recvs.append(exchange(send, self.scheme[0][1]))
        self.calls.follows(send)

    def keep_first(self, keep):
        self.pairs.append((keep, self.recvs.pop(0)))

    def step(self):
        stage, calls = self.stage, self.calls
        name = f"sum_{self.name}{stage}"
        kind, bits = self.scheme[stage]
        if stage + 1 == len(self.scheme):
            sent = self.recv
            if "g" + self.name in PLAN:
                (sent,) = calls(copy_kernel, name, [(sent.shape, bf16, "v")], [(sent, "v")])
            self.others.append(swap_cores(sent))
            calls.also += [sent, self.others[0]]
            self.quarters = [(v, "v") for v in (self.send, self.recv, *self.others)]
            return
        next_kind, next_bits = self.scheme[stage + 1]
        pairs = self.pairs if stage == 0 else [(self.keep, self.recv)]
        ins = [(v, "v") for pair in pairs for v in pair]
        rows, width = sum(p[0].shape[0] for p in pairs), pairs[0][1].shape[1]
        if next_kind == "halve":
            half = ((rows // 2, width), bf16, "v")
            self.keep, self.send = calls(
                functools.partial(split_kernel, PLACE_OF[next_bits]), name, [half, half], ins,
                scratch=[pltpu.VMEM((rows, width), bf16)] if len(pairs) > 1 else [],
            )
        else:
            small = self.small if kind == "halve" and self.small is not None else None
            behind = SMALL_ROWS if self.small is not None else 0
            if kind == "join":
                h = rows - behind
                kernel, rows = functools.partial(join_kernel, h, PLACE_OF[bits]), 2 * h + behind
            else:
                kernel = sum_kernel
                if small is not None:
                    ins.append((small, "v"))
                    rows += behind
            (self.send,) = calls(kernel, name, [((rows, width), bf16, "v")], ins)
            count = lax.axis_size("batch")
            if kind != "join" and next_kind == "join" and count > 16:
                others = [[j + 16 * i for i in range(count // 16)] for j in range(16)]
                self.send = lax.psum(self.send, "batch", axis_index_groups=others)
            self.keep = self.send
        self.stage += 1
        self.recv = exchange(self.send, next_bits)
        calls.follows(self.send)
        if self.stage + 1 == len(self.scheme):
            self.others = [swap_cores(self.send)]


CONV_BLOCKS = (5, 4)
GROUPS = {"a": "a", "b": "b", "c": "c", "d": "d"}
SCHEMES = {"a": SHORT, "b": SHORT, "c": LONG, "d": LONG}
PLAN = (
    "R0", "R1", "F", "a", "b", "Dcs", "a", "Dck", "Dds", "b", "Ddk", "c", "a", "E0", "d", "c", "b", "E1", "a",
    "d", "c", "S", "b", "d", "a", "c", "b", "a", "d", "c", "b", "d", "c", "fb", "d", "gc", "fa", "gd", "c",
    "d", "fc", "fd",
)


def body(
    inputs,
    conv_weight,
    conv_bias,
    norm1_gain,
    norm1_shift,
    norm2_gain,
    norm2_shift,
    up_weight,
    up_bias,
    down_weight,
    down_bias,
    head_weight,
    species,
    cotangent,
):
    nw, seg, d = inputs.shape
    taps = conv_weight.shape[0]
    ff = up_weight.shape[1]
    rows = nw * seg
    rim = (taps - 1) // 2 * DILATION_STEP
    calls = Calls()
    head = head_weight.T
    ub = up_bias.reshape(1, ff)
    xp = swap_cores(inputs)
    win = (nw, seg, d)
    sides = ((2, nw, seg + 2 * rim, d), bf16, "v")
    six = [v.reshape(1, d) for v in (conv_bias, norm1_gain, norm1_shift, norm2_gain, norm2_shift, down_bias)]
    a, both, w, x, vectors = calls(
        functools.partial(prepare_kernel, rim),
        "prepare",
        [((nw, 2 * seg, d), bf16, "v"), sides, (conv_weight.shape, bf16, "v"), (win, bf16, "v"), ((8, d), f32, "v")],
        [(v, "a") for v in (inputs, conv_weight, *six)],
        scratch=[pltpu.VMEM((nw, seg + 2 * rim, d), f32), pltpu.SemaphoreType.DMA((6 + nw + taps,))],
    )
    h, gp, n, dy, up, down, _ = calls(
        functools.partial(conv_kernel, rim),
        "conv_forward",
        [
            (win, f32, "v"), (win, f32, "v"), (win, bf16, "v"), (win, bf16, "v"),
            (up_weight.shape, bf16, "v"), (down_weight.shape, bf16, "v"), sides,
        ],
        [(v, "v") for v in (xp, both, w, x, vectors)] + [(v, "a") for v in (cotangent, up_weight, down_weight)],
        scratch=[pltpu.SemaphoreType.DMA((3,))],
        aliases={1: 6},
    )
    h, gp, n, dyr = (v.reshape(rows, d) for v in (h, gp, n, dy))

    wide = ((rows, FF_BLOCK), bf16, "v")
    recvs = []
    groups = {name: Group(name, calls, SCHEMES[name]) for name in GROUPS}
    owner = {member: groups[name] for name, members in GROUPS.items() for member in members}
    starts = {members[i]: i * FF_BLOCK for members in GROUPS.values() for i in range(len(members))}
    qs, dzs = [], []
    ubg = None
    for index in range(4):
        ins = [n, dyr, up, ub, down]
        if index >= 2:
            ins.append(recvs[index - 2])
        if index:
            ins.append(ubg)
        outs = [((FF_BLOCK, d), bf16, "v")] * 2 if index >= 2 else [((2 * FF_BLOCK, d), bf16, "v")]
        *res, q, dz, ubg = calls(
            functools.partial(ffn_kernel, index),
            f"ffn_{index}",
            outs + [wide, wide, ((1, ff), f32, "v")],
            [(v, "v") for v in ins],
            scratch=[pltpu.VMEM((2 * FF_BLOCK, d), f32)],
            limit=8,
        )
        qs.append(q)
        dzs.append(dz)
        if index >= 2:
            owner["ab"[index - 2]].send_first(res[1])
            owner["ab"[index - 2]].keep_first(res[0])
        else:
            recvs.append(swap_cores(res[0]))
            calls.follows(res[0])
    after = []

    bases = {"c": 0, "d": 2 * CONV_BLOCKS[0]}
    assert 2 * sum(CONV_BLOCKS) == 2 * taps
    half = d // 2
    extent = 2 * seg + 2 * rim
    both = None
    input_grad = sums1 = None
    final = {}
    for item in PLAN:
        if item[0] == "R":
            ins = [dyr, up, down, h, gp, vectors, *qs, *dzs]
            outs = [((rows, d), bf16, "v"), ((rows, d), f32, "v"), ((rows, d), bf16, "v"), ((4, d), f32, "v")]
            if item == "R0":
                aliases = {len(ins) + 1: 4}
                ins += [xp, a]
                outs.append((a.shape, bf16, "v"))
            else:
                aliases = {len(ins) + i: i for i in range(4)}
                ins += after
            *after, last = calls(
                functools.partial(rows_kernel, int(item[1])), f"rows_{item[1]}", outs, [(v, "v") for v in ins], aliases=aliases
            )
            if item == "R0":
                a = last
            else:
                act, dh, du = after
                sums2 = last
                du, dh = du.reshape(win), dh.reshape(win)
                dup = swap_cores(du)
                calls.follows(du)
        elif item == "F":
            act_out, freq = calls(
                head_kernel,
                "head",
                [((rows, d), bf16, "a"), ((SPECIES, 128), f32, "v")],
                [(act, "v"), (head, "v"), (species.reshape(1, nw), "v")],
                scratch=[pltpu.SemaphoreType.DMA((1,)), pltpu.VMEM((128, d), bf16)],
            )
        elif item[0] == "D":
            g = item[1]
            blocks = CONV_BLOCKS["cd".index(g)]
            kernel = functools.partial(conv_weight_kernel, rim, bases[g], blocks, item[2] == "k", both is None)
            outs = [((blocks * half, half), bf16, "v")]
            ins = [(a, "v"), (du, "v"), (dup, "v")]
            if both is None:
                outs.append(((2, nw, extent, half), bf16, "v"))
                part, both = calls(kernel, f"conv_weight_{item}", outs, ins, scratch=[pltpu.VMEM((extent, half), f32)] * nw)
            else:
                (part,) = calls(kernel, f"conv_weight_{item}", outs, ins + [(both, "v")])
            if item[2] == "s":
                owner[g].send_first(part)
            else:
                owner[g].keep_first(part)
        elif item[0] == "E":
            windows = (0, 1) if item == "E0" else (2, 3)
            ins = [(du, "v"), (dup, "v"), (conv_weight, "a") if item == "E0" else (w, "v"), (dh, "v"), (x, "v"), (vectors, "v")]
            outs = [(win, bf16, "a"), ((2, d), f32, "v")]
            aliases = None
            if item == "E0":
                outs.append((conv_weight.shape, bf16, "v"))
            else:
                aliases = {len(ins): 0}
                ins += [(input_grad, "a"), (sums1, "v")]
            input_grad, sums1, *more = calls(
                functools.partial(conv_input_kernel, rim, windows),
                f"conv_input_{windows[0]}",
                outs,
                ins,
                scratch=[pltpu.VMEM((2, seg, d), bf16), pltpu.SemaphoreType.DMA((2 + taps,))]
                + window_scratch(2, seg, rim, d),
                limit=12,
                aliases=aliases,
            )
            if more:
                (w,) = more
        elif item == "S":
            (owner["d"].small,) = calls(
                small_kernel, "small", [((SMALL_ROWS, half), f32, "v")], [(sums2, "v"), (sums1, "v"), (ubg, "v"), (freq, "v")]
            )
        elif item[0] in "fg":
            g = owner[item[1]]
            if item[1] in "ab":
                prev = final.get("ffn", ())[:2]
                final["ffn"] = calls(
                    functools.partial(final_ffn_kernel, "ab".index(item[1]), starts[item[1]]),
                    f"final_{item[1]}",
                    [(down_weight.shape, f32, "a"), (up_weight.shape, f32, "a"), MARK],
                    g.quarters + [(p, "a") for p in prev],
                    scratch=[pltpu.VMEM((4, FF_BLOCK, d), f32), pltpu.SemaphoreType.DMA((8,))],
                    limit=10,
                    aliases={4 + i: i for i in range(len(prev))},
                )
            else:
                prev = final.get("conv", ())[:1]
                early, last = item[0] == "g", item[1] == "d" and item[0] == "f"
                chosen = (0, 2) if early else (1, 3) if "g" + item[1] in PLAN else (0, 1, 2, 3)
                small = [d] * 6 + [ff] if last else []
                outs = [((taps * d, d), f32, "a")] + [((1, k), f32, "a") for k in small]
                outs += [((SPECIES, head_weight.shape[1]), f32, "a")] if small else []
                outs.append(MARK)
                more = [pltpu.VMEM((len(small), ff), f32), pltpu.VMEM((SPECIES, head_weight.shape[1]), f32)] if small else []
                quarters = [(g.send, "v"), (g.send, "v"), (g.others[0], "v"), (g.others[0], "v")] if early else g.quarters
                final["conv"] = calls(
                    functools.partial(final_conv_kernel, bases[item[1]] * half, chosen, len(small)),
                    f"final_{item}",
                    outs,
                    quarters + [(p, "a") for p in prev],
                    scratch=[
                        pltpu.VMEM((4, CONV_BLOCKS["cd".index(item[1])] * half, half), f32),
                        pltpu.SemaphoreType.DMA((5 + len(small),)),
                    ]
                    + more,
                    limit=10,
                    aliases={4: 0} if prev else None,
                )
        else:
            groups[item].step()
    down_grad, up_grad, _ = final["ffn"]
    conv_grad, conv_b, g2, s2, down_b, g1, s1, up_b, frequencies, _ = final["conv"]
    return (
        act_out.reshape(win),
        input_grad,
        conv_grad.reshape(taps, d, d),
        conv_b.reshape(d),
        g1.reshape(d),
        s1.reshape(d),
        g2.reshape(d),
        s2.reshape(d),
        up_grad,
        up_b.reshape(ff),
        down_grad,
        down_b.reshape(d),
        frequencies,
    )


def solution(mesh):
    rows = P("batch", "seq", None)
    placed = (rows,) + (P(),) * 11 + (P("batch"), rows)
    return jax.shard_map(
        body, mesh=mesh, in_specs=placed, out_specs=(rows, rows) + (P(),) * 11, check_vma=False
    )
```
